32 devices in a mesh: seq: 16 (over z, y, x), head: 2 (over core).
Axes of the slice: x: 2, y: 2, z: 4, core: 2. Of those that a mesh axis runs over, the one named last changes fastest.
Arguments:
- x_in: bfloat16 [2, 4096, 1536], P(None, 'seq'), may hold values from -6 to 6
- cotangent: bfloat16 [2, 4096, 1536], P(None, 'seq'), may hold values from -6 to 6
- cond: bfloat16 [2, 8, 1536], replicated, may hold values from -6 to 6
- context: bfloat16 [2, 8, 128, 768], replicated, may hold values from -6 to 6
- clip_lengths: int32 [2, 8], replicated, may hold values from 204 to 2048, as said below
- pad_mask: int32 [2, 4096], replicated, may hold values 0 or 1
- owners: int32 [2, 1800], P('head'), may hold values from 0 to 15, as said below
- master: float32 [2, 2256, 128, 128], P('head', 'seq'), may hold values from -4 to 4, as said below
- first_moment: float32 [2, 2256, 128, 128], P('head', 'seq'), may hold values from -1048576 to 1048576
- second_moment: float32 [2, 2256, 128, 128], P('head', 'seq'), may hold values from 0 to 1048576, as said below
Outputs:
- out_block: bfloat16 [2, 4096, 1536], P(None, 'seq')
- grad_input: float32 [2, 4096, 1536], P(None, 'seq')
- new_master: float32 [2, 2256, 128, 128], P('head', 'seq')
- new_first: float32 [2, 2256, 128, 128], P('head', 'seq')
- new_second: float32 [2, 2256, 128, 128], P('head', 'seq')
The draws below stay inside these ranges and needn't reach their ends.
Inputs may be any that keep to these rules, and one draw needn't show every extreme that they name: `clip_lengths`: the clips of a micro-batch fill its 4096 frames; each clip has 204 frames or more, and in every micro-batch one clip has exactly 2048. `owners`: every tile of a head shard has one owner; no owner holds more than 141 tiles of one shard, and in each shard one owner holds exactly 141. `master`: slots that hold no tile carry finite values. `second_moment`: every entry is positive.
All inputs are finite; a program needn't handle non-finite values.
Results may differ from the reference program's by a relative error of at most 0.035.
Values may be sent and summed in bfloat16 or wider, within the bound.
No kernel may reach another device: no remote copies, remote signals or barrier semaphores. Data moves between devices by JAX's collectives and lax.ppermute only.
A program may use at most 768 MiB of HBM per device.

```python
import jax
import jax.numpy as jnp
import numpy as np
from jax import lax

D = 1536
HEADS = 24
HD = 64
FF = 6144
DC = 768
CTX = 128
TOK_DEV = 256
MICRO = 2
WIN = 128
TS = 128
STEP = 5
NCLIP = 8
FRAMES = 4096
MAXLEN = 2048
MINLEN = 204
NT = 1800
CAP = 141
N_SEQ = 16
N_HEAD = 2


def owner_table(key):
    shard_rows = []
    for shard_idx in range(N_HEAD):
        base_key = jax.random.fold_in(key, 700 + shard_idx)
        busiest = jax.random.randint(jax.random.fold_in(base_key, 1), (), 0, N_SEQ)
        chosen = jax.random.permutation(jax.random.fold_in(base_key, 2), (N_SEQ - 1) * CAP)[:NT - CAP]
        others = (busiest + 1 + chosen // CAP) % N_SEQ
        listed = jnp.concatenate([jnp.full((CAP,), busiest, jnp.int32), others.astype(jnp.int32)])
        shard_rows.append(jax.random.permutation(jax.random.fold_in(base_key, 3), listed))
    return jnp.stack(shard_rows).astype(jnp.int32)


def tile_counts():
    head_cols = D // N_HEAD
    ff_cols = FF // N_HEAD
    piece_sizes = [D * 3 * head_cols, head_cols * D, D * head_cols, DC * 2 * head_cols, head_cols * D, D * 2 * ff_cols, ff_cols * D, D * 6 * D // N_HEAD]
    return [piece_size // (TS * TS) for piece_size in piece_sizes]


def slot_kinds(key):
    owners = owner_table(key)
    kind_ends = jnp.array([int(end_value) for end_value in np.cumsum(tile_counts())[:-1]], dtype=jnp.int32)
    shard_rows = []
    for shard_idx in range(N_HEAD):
        owner_row = owners[shard_idx]
        onehot = (owner_row[:, None] == jnp.arange(N_SEQ, dtype=jnp.int32)[None, :]).astype(jnp.int32)
        before = jnp.cumsum(onehot, axis=0) - onehot
        tile_place = owner_row * CAP + jnp.sum(before * onehot, axis=1)
        slot_tile = jnp.full((N_SEQ * CAP,), -1, jnp.int32).at[tile_place].set(jnp.arange(NT, dtype=jnp.int32))
        shard_rows.append(jnp.sum((slot_tile[:, None] >= kind_ends[None, :]).astype(jnp.int32), axis=1))
    return jnp.stack(shard_rows)


def kind_scale(slot_kind, scale_list):
    onehot = (slot_kind[..., None] == jnp.arange(len(scale_list), dtype=jnp.int32)).astype(jnp.float32)
    return jnp.sum(onehot * jnp.array(scale_list, jnp.float32), axis=-1)[..., None, None]


def grad_sizes():
    root_tokens = (MICRO * TOK_DEV * N_SEQ) ** 0.5
    return [1.5 * root_tokens, 0.12 * root_tokens, 1.7 * root_tokens, 0.15 * root_tokens * CTX ** 0.5, 0.15 * root_tokens, 0.5 * root_tokens, 0.6 * root_tokens, 1.4 * root_tokens]


def draw_clip_lengths(key, part):
    key = jax.random.fold_in(key, 21)
    rows = []
    other_count = NCLIP - 1
    for micro_idx in range(MICRO):
        micro_key = jax.random.fold_in(key, micro_idx)
        shares = jax.random.randint(jax.random.fold_in(micro_key, 1), (other_count,), 2, 5).astype(jnp.int32)
        remain = FRAMES - MAXLEN - other_count * MINLEN
        portion = remain * shares // jnp.sum(shares)
        leftover = remain - jnp.sum(portion)
        extra = (jnp.arange(other_count, dtype=jnp.int32) < leftover).astype(jnp.int32)
        others = (MINLEN + portion + extra).astype(jnp.int32)
        spot = jax.random.randint(jax.random.fold_in(micro_key, 2), (), 0, NCLIP)
        index = jnp.arange(NCLIP, dtype=jnp.int32)
        other_index = jnp.clip(index - (index > spot).astype(jnp.int32), 0, other_count - 1)
        rows.append(jnp.where(index == spot, MAXLEN, others[other_index]).astype(jnp.int32))
    return jnp.stack(rows).astype(jnp.int32)


def draw_owners(key, part):
    return owner_table(key)


def draw_master(key, part):
    slot_kind = slot_kinds(key)
    key = jax.random.fold_in(key, 11)
    normal_draw = jnp.clip(jax.random.normal(key, (N_HEAD, N_SEQ * CAP, TS, TS), jnp.float32), -4.0, 4.0)
    fan_list = [D, D // 64, D, DC, D // 32, D, FF // 4, 4 * D]
    return normal_draw * kind_scale(slot_kind, [fan_in ** (-0.5) for fan_in in fan_list])


def draw_first_moment(key, part):
    slot_kind = slot_kinds(key)
    key = jax.random.fold_in(key, 12)
    normal_draw = jnp.clip(jax.random.normal(key, (N_HEAD, N_SEQ * CAP, TS, TS), jnp.float32), -4.0, 4.0)
    return normal_draw * kind_scale(slot_kind, [0.111 * grad_size for grad_size in grad_sizes()])


def draw_second_moment(key, part):
    slot_kind = slot_kinds(key)
    key = jax.random.fold_in(key, 13)
    spread = jnp.exp(jax.random.uniform(key, (N_HEAD, N_SEQ * CAP, TS, TS), jnp.float32, np.log(0.5), np.log(2.0)))
    return 2.0 * spread * kind_scale(slot_kind, [0.0526 * grad_size * grad_size for grad_size in grad_sizes()])


def plant(values, key, least, top_value):
    longest = values.shape.index(max(values.shape))
    spots = []
    for shift in (0, 1):
        where = [jax.random.randint(jax.random.fold_in(key, axis), (), 0, length) for axis, length in enumerate(values.shape)]
        where[longest] = (where[longest] + shift) % values.shape[longest]
        spots.append(tuple(where))
    return values.at[spots[0]].set(least).at[spots[1]].set(top_value)


def steps_of(own_key, shape, cuts, smallest, largest):
    factor_of = 1.0
    for axis_at, blocks in cuts:
        steps = jax.random.uniform(jax.random.fold_in(jax.random.fold_in(own_key, 6), axis_at), (blocks,), jnp.float32, smallest / len(cuts), largest / len(cuts))
        factor_of = factor_of * jnp.repeat(jnp.exp(steps), shape[axis_at] // blocks).reshape((-1,) + (1,) * (len(shape) - 1 - axis_at))
    return factor_of


def bell_draw(key, dims, width, most, split=(), kind=jnp.bfloat16):
    values = width * jax.random.normal(key, dims, jnp.float32)
    if split:
        values = values * steps_of(key, dims, split, -0.22, 0.18)
    return jnp.clip(values, -most, most).astype(kind)


def setup_inputs(seed: int = 0) -> dict:
    splits = jax.random.split(jax.random.key(seed), 11)
    return {
        "x_in": bell_draw(splits[0], (MICRO, FRAMES, D), 1.0, 6.0, ((1, 16),)),
        "cotangent": bell_draw(splits[1], (MICRO, FRAMES, D), 1.0, 6.0, ((1, 16),)),
        "cond": bell_draw(splits[2], (MICRO, NCLIP, D), 1.0, 6.0),
        "context": bell_draw(splits[3], (MICRO, NCLIP, CTX, DC), 1.0, 6.0),
        "clip_lengths": draw_clip_lengths(jax.random.fold_in(splits[10], 71), 0),
        "pad_mask": plant((jax.random.randint(splits[5], (MICRO, FRAMES), 0, 4) < 3).astype(jnp.int32), jax.random.fold_in(splits[5], 1), 0, 1),
        "owners": draw_owners(jax.random.fold_in(splits[10], 71), 0),
        "master": draw_master(jax.random.fold_in(splits[10], 71), 0),
        "first_moment": draw_first_moment(jax.random.fold_in(splits[10], 71), 0),
        "second_moment": draw_second_moment(jax.random.fold_in(splits[10], 71), 0),
    }


PRECISE = lax.Precision.HIGHEST
EPS_NORM = 1e-06
BETA_ONE = 0.9
BETA_TWO = 0.95
ADAM_EPS = 1e-08
WEIGHT_DECAY = 0.1
LEARN_RATE = 0.5
MASKED = -1e+30

@jax.custom_vjp
def low(v):
    return lax.optimization_barrier(v.astype(jnp.bfloat16)).astype(jnp.float32)

@jax.custom_vjp
def low_back(v):
    return v

def low_keep(v):
    return (low(v), None)

def low_pass(kept, grad):
    return (grad,)

def back_keep(v):
    return (v, None)

def back_low(kept, grad):
    return (low(grad),)
low.defvjp(low_keep, low_pass)
low_back.defvjp(back_keep, back_low)

def piece_shapes():
    head_cols = D // N_HEAD
    ff_cols = FF // N_HEAD
    return [(D, 3 * head_cols), (head_cols, D), (D, head_cols), (DC, 2 * head_cols), (head_cols, D), (D, 2 * ff_cols), (ff_cols, D), (D, 6 * D // N_HEAD)]

def fan_inputs():
    return [D, D // 64, D, DC, D // 32, D, FF // 4, 4 * D]

def slot_layout(owner_row, seq_count, capacity):
    onehot = (owner_row[:, None] == jnp.arange(seq_count, dtype=jnp.int32)[None, :]).astype(jnp.int32)
    before = jnp.cumsum(onehot, axis=0) - onehot
    tile_place = (owner_row * capacity + lax.optimization_barrier(jnp.sum(before * onehot, axis=1))).astype(jnp.int32)
    tile_count = owner_row.shape[0]
    slot_tile = jnp.full((seq_count * capacity,), -1, jnp.int32).at[tile_place].set(jnp.arange(tile_count, dtype=jnp.int32))
    return (tile_place, slot_tile)

def slot_rates(slot_tile, shapes):
    counts = [row_count * col_count // (TS * TS) for row_count, col_count in shapes]
    kind_ends = jnp.array([int(end_value) for end_value in np.cumsum(counts)[:-1]], dtype=jnp.int32)
    slot_kind = lax.optimization_barrier(jnp.sum((slot_tile[:, None] >= kind_ends[None, :]).astype(jnp.int32), axis=1))
    rate_table = jnp.array([LEARN_RATE * fan_in ** (-0.5) for fan_in in fan_inputs()], dtype=jnp.float32)
    onehot = (slot_kind[:, None] == jnp.arange(len(shapes), dtype=jnp.int32)[None, :]).astype(jnp.float32)
    return lax.optimization_barrier(jnp.sum(onehot * rate_table[None, :], axis=1))

def split_pieces(flattened, shapes):
    pieces = []
    offset = 0
    for row_count, col_count in shapes:
        pieces.append(flattened[offset:offset + row_count * col_count].reshape(row_count, col_count))
        offset = offset + row_count * col_count
    return pieces

def layer_norm(values):
    centred = values - lax.optimization_barrier(jnp.mean(values, axis=-1, keepdims=True))
    return centred * lax.rsqrt(lax.optimization_barrier(jnp.mean(centred * centred, axis=-1, keepdims=True)) + EPS_NORM)

def clip_ids(lengths, positions):
    clip_ends = jnp.cumsum(lengths)
    return lax.optimization_barrier(jnp.sum((positions[:, None] >= clip_ends[None, :]).astype(jnp.int32), axis=1))

def window_mask(query_pos, key_pos, key_flag, lengths, frames):
    query_clip = clip_ids(lengths, query_pos)
    key_clip = clip_ids(lengths, key_pos)
    offset = key_pos[None, :] - query_pos[:, None]
    is_near = (offset <= WIN) & (offset >= -WIN)
    is_inside = (key_pos >= 0) & (key_pos < frames)
    same_clip = query_clip[:, None] == key_clip[None, :]
    is_kept = (key_flag[None, :] == 1) | (offset == 0)
    return is_near & is_inside[None, :] & same_clip & is_kept

def self_attention(queries, keys, values, lengths, mask_row):
    frames = queries.shape[0]
    block_rows = 512 if frames % 512 == 0 else frames
    key_pad = jnp.pad(keys, ((WIN, WIN), (0, 0), (0, 0)))
    value_pad = jnp.pad(values, ((WIN, WIN), (0, 0), (0, 0)))
    mask_pad = jnp.pad(mask_row, (WIN, WIN))
    scale = HD ** (-0.5)

    def one_block(first_row):
        query_block = lax.dynamic_slice_in_dim(queries, first_row, block_rows, 0)
        key_block = lax.dynamic_slice_in_dim(key_pad, first_row, block_rows + 2 * WIN, 0)
        value_block = lax.dynamic_slice_in_dim(value_pad, first_row, block_rows + 2 * WIN, 0)
        flag_block = lax.dynamic_slice_in_dim(mask_pad, first_row, block_rows + 2 * WIN, 0)
        query_pos = first_row + jnp.arange(block_rows, dtype=jnp.int32)
        key_pos = first_row - WIN + jnp.arange(block_rows + 2 * WIN, dtype=jnp.int32)
        allowed = window_mask(query_pos, key_pos, flag_block, lengths, frames)
        scores = low_back(scale * jnp.einsum('qhd,khd->hqk', query_block, key_block, precision=PRECISE))
        scores = jnp.where(allowed[None], scores, MASKED)
        probs = jax.nn.softmax(scores, axis=-1)
        return jnp.einsum('hqk,khd->qhd', low(probs), value_block, precision=PRECISE)
    starts = jnp.arange(frames // block_rows, dtype=jnp.int32) * block_rows
    result = lax.map(jax.checkpoint(one_block), starts)
    return result.reshape(frames, -1)

def cross_attention(queries, keys, values, clip_tok):
    frames = queries.shape[0]
    block_rows = 512 if frames % 512 == 0 else frames
    key_clip = jnp.arange(keys.shape[0], dtype=jnp.int32) // CTX
    scale = HD ** (-0.5)

    def one_block(first_row):
        query_block = lax.dynamic_slice_in_dim(queries, first_row, block_rows, 0)
        clip_block = lax.dynamic_slice_in_dim(clip_tok, first_row, block_rows, 0)
        scores = low_back(scale * jnp.einsum('qhd,khd->hqk', query_block, keys, precision=PRECISE))
        scores = jnp.where((clip_block[:, None] == key_clip[None, :])[None], scores, MASKED)
        probs = jax.nn.softmax(scores, axis=-1)
        return jnp.einsum('hqk,khd->qhd', low(probs), values, precision=PRECISE)
    starts = jnp.arange(frames // block_rows, dtype=jnp.int32) * block_rows
    result = lax.map(jax.checkpoint(one_block), starts)
    return result.reshape(frames, -1)

def block(resid, cond_row, ctx_row, lengths, mask_row, weights):
    frames = resid.shape[0]
    head_cols = D // N_HEAD
    ff_cols = FF // N_HEAD
    positions = jnp.arange(frames, dtype=jnp.int32)
    clip_tok = clip_ids(lengths, positions)
    mod_weight = jnp.concatenate([pieces[7] for pieces in weights], axis=1)
    modulation = jnp.dot(cond_row, mod_weight, precision=PRECISE)
    onehot = (clip_tok[:, None] == jnp.arange(NCLIP, dtype=jnp.int32)[None, :]).astype(resid.dtype)
    mod_frames = jnp.dot(onehot, modulation, precision=PRECISE)

    def modulate(values, which):
        shift_part = mod_frames[:, 2 * which * D:(2 * which + 1) * D]
        scale_part = mod_frames[:, (2 * which + 1) * D:(2 * which + 2) * D]
        return layer_norm(values) * (1.0 + scale_part) + shift_part
    normed_one = low(modulate(resid, 0))
    proj_qkv = [low(low_back(jnp.dot(normed_one, pieces[0], precision=PRECISE))) for pieces in weights]
    queries = jnp.concatenate([part[:, :head_cols] for part in proj_qkv], axis=1).reshape(frames, HEADS, HD)
    keys = jnp.concatenate([part[:, head_cols:2 * head_cols] for part in proj_qkv], axis=1).reshape(frames, HEADS, HD)
    values = jnp.concatenate([part[:, 2 * head_cols:] for part in proj_qkv], axis=1).reshape(frames, HEADS, HD)
    attended = low(low_back(self_attention(queries, keys, values, lengths, mask_row)))
    first_sum = resid + sum((low(low_back(jnp.dot(attended[:, shard_idx * head_cols:(shard_idx + 1) * head_cols], weights[shard_idx][1], precision=PRECISE))) for shard_idx in range(N_HEAD)))
    normed_two = low(modulate(first_sum, 1))
    cross_queries = jnp.concatenate([low(low_back(jnp.dot(normed_two, pieces[2], precision=PRECISE))) for pieces in weights], axis=1).reshape(frames, HEADS, HD)
    ctx_flat = ctx_row.reshape(NCLIP * CTX, DC)
    cross_proj = [low(jnp.dot(ctx_flat, pieces[3], precision=PRECISE)) for pieces in weights]
    cross_keys = jnp.concatenate([part[:, :head_cols] for part in cross_proj], axis=1).reshape(NCLIP * CTX, HEADS, HD)
    cross_values = jnp.concatenate([part[:, head_cols:] for part in cross_proj], axis=1).reshape(NCLIP * CTX, HEADS, HD)
    cross_out = low(low_back(cross_attention(cross_queries, cross_keys, cross_values, clip_tok)))
    second_sum = first_sum + sum((low(low_back(jnp.dot(cross_out[:, shard_idx * head_cols:(shard_idx + 1) * head_cols], weights[shard_idx][4], precision=PRECISE))) for shard_idx in range(N_HEAD)))
    normed_three = low(modulate(second_sum, 2))
    total = second_sum
    for pieces in weights:
        gate_up = low_back(jnp.dot(normed_three, pieces[5], precision=PRECISE))
        gate_part = gate_up[:, :ff_cols]
        up_part = gate_up[:, ff_cols:]
        hidden = low(jax.nn.silu(gate_part) * up_part)
        total = total + low(low_back(jnp.dot(hidden, pieces[6], precision=PRECISE)))
    return total

def adam_step(weight, first, second, grads, rate):
    first = BETA_ONE * first + (1.0 - BETA_ONE) * grads
    second = BETA_TWO * second + (1.0 - BETA_TWO) * grads * grads
    first_hat = first / (1.0 - BETA_ONE ** STEP)
    second_hat = second / (1.0 - BETA_TWO ** STEP)
    weight = weight - rate * (first_hat / (jnp.sqrt(second_hat) + ADAM_EPS) + WEIGHT_DECAY * weight)
    return (weight, first, second)

def reference(x_in, cotangent, cond, context, clip_lengths, pad_mask, owners, master, first_moment, second_moment):
    shapes = piece_shapes()
    layouts = [slot_layout(owners[shard_idx], N_SEQ, CAP) for shard_idx in range(N_HEAD)]
    weights = []
    for shard_idx in range(N_HEAD):
        tile_rows = master[shard_idx][layouts[shard_idx][0]]
        weights.append(split_pieces(low(tile_rows.reshape(-1)), shapes))
    cond_f = cond.astype(jnp.float32)
    ctx_f = context.astype(jnp.float32)

    def forward(x_all, params):
        return jnp.stack([block(x_all[micro_idx], cond_f[micro_idx], ctx_f[micro_idx], clip_lengths[micro_idx], pad_mask[micro_idx], params) for micro_idx in range(MICRO)])
    result, pullback = jax.vjp(forward, x_in.astype(jnp.float32), weights)
    grad_x, grad_w = pullback(cotangent.astype(jnp.float32))
    new_w, new_m, new_v = ([], [], [])
    for shard_idx in range(N_HEAD):
        tile_place, slot_tile = layouts[shard_idx]
        flattened = jnp.concatenate([piece.reshape(-1) for piece in grad_w[shard_idx]])
        grad_tiles = flattened.reshape(-1, TS, TS)
        grad_slots = jnp.zeros((N_SEQ * CAP, TS, TS), jnp.float32).at[tile_place].set(grad_tiles)
        rate = slot_rates(slot_tile, shapes)[:, None, None]
        weight, first, second = adam_step(master[shard_idx], first_moment[shard_idx], second_moment[shard_idx], grad_slots, rate)
        new_w.append(weight)
        new_m.append(first)
        new_v.append(second)
    return (result.astype(jnp.bfloat16), grad_x, jnp.stack(new_w), jnp.stack(new_m), jnp.stack(new_v))
```

```python
import math
from functools import partial

import jax
import jax.numpy as jnp
import numpy as np
from jax import lax
from jax.experimental import pallas as pl
from jax.experimental.pallas import tpu as pltpu
from jax.sharding import PartitionSpec as P

D = 1536
HD = 64
FF = 6144
DC = 768
CTX = 128
WIN = 128
TS = 128
STEP = 5
MINLEN = 204


PRECISE = lax.Precision.HIGHEST
EPS_NORM = 1e-06
BETA_ONE = 0.9
BETA_TWO = 0.95
ADAM_EPS = 1e-08
WEIGHT_DECAY = 0.1
LEARN_RATE = 0.5
MASKED = -1e30


def padded(shard, sides, width):
    for axis, dim in sides:
        size, length = (lax.axis_size(axis), shard.shape[dim])
        up = [(i, (i + 1) % size) for i in range(size - 1)]
        down = [(j, i) for i, j in up]
        last = lax.slice_in_dim(shard, length - width, length, axis=dim)
        initial = lax.slice_in_dim(shard, 0, width, axis=dim)
        before = lax.ppermute(last, axis, up)
        after = lax.ppermute(initial, axis, down)
        shard = jnp.concatenate([before, shard, after], axis=dim)
    return shard


def piece_shapes(head_count):
    head_cols = D // head_count
    ff_cols = FF // head_count
    return [
        (D, 3 * head_cols),
        (head_cols, D),
        (D, head_cols),
        (DC, 2 * head_cols),
        (head_cols, D),
        (D, 2 * ff_cols),
        (ff_cols, D),
        (D, 6 * D // head_count),
    ]


def fan_inputs():
    return [D, D // 64, D, DC, D // 32, D, FF // 4, 4 * D]


def slot_rates(slot_tile, shapes):
    counts = [row_count * col_count // (TS * TS) for row_count, col_count in shapes]
    kind_ends = jnp.array([int(end_value) for end_value in np.cumsum(counts)[:-1]], dtype=jnp.int32)
    slot_kind = jnp.sum((slot_tile[:, None] >= kind_ends[None, :]).astype(jnp.int32), axis=1)
    rate_table = jnp.array(
        [LEARN_RATE * fan_in ** (-0.5) for fan_in in fan_inputs()], dtype=jnp.float32
    )
    onehot = (slot_kind[:, None] == jnp.arange(len(shapes), dtype=jnp.int32)[None, :]).astype(
        jnp.float32
    )
    return jnp.sum(onehot * rate_table[None, :], axis=1)


def split_pieces(flattened, shapes):
    pieces = []
    offset = 0
    for row_count, col_count in shapes:
        pieces.append(
            flattened[offset : offset + row_count * col_count].reshape(row_count, col_count)
        )
        offset = offset + row_count * col_count
    return pieces


def layer_norm(values):
    centred = values - jnp.mean(values, axis=-1, keepdims=True)
    inverse = lax.rsqrt(jnp.mean(centred * centred, axis=-1, keepdims=True) + EPS_NORM)
    return (centred * inverse, inverse)


def norm_back(grad, normed, inverse, scale_part):
    dnormed = grad * (1.0 + scale_part)
    dvalues = inverse * (
        dnormed
        - jnp.mean(dnormed, axis=-1, keepdims=True)
        - normed * jnp.mean(dnormed * normed, axis=-1, keepdims=True)
    )
    return (dvalues, grad * normed, grad)


def clip_ids(lengths, positions):
    clip_ends = jnp.cumsum(lengths)
    return jnp.sum((positions[:, None] >= clip_ends[None, :]).astype(jnp.int32), axis=1)


def window_mask(query_pos, key_pos, key_flag, lengths, frames):
    query_clip = clip_ids(lengths, query_pos)
    key_clip = clip_ids(lengths, key_pos)
    offset = key_pos[None, :] - query_pos[:, None]
    is_near = (offset <= WIN) & (offset >= -WIN)
    is_inside = (key_pos >= 0) & (key_pos < frames)
    same_clip = query_clip[:, None] == key_clip[None, :]
    is_kept = (key_flag[None, :] == 1) | (offset == 0)
    return is_near & is_inside[None, :] & same_clip & is_kept


def adam_step(weight, first, second, grads, rate):
    first = BETA_ONE * first + (1.0 - BETA_ONE) * grads
    second = BETA_TWO * second + (1.0 - BETA_TWO) * grads * grads
    first_hat = first / (1.0 - BETA_ONE**STEP)
    second_hat = second / (1.0 - BETA_TWO**STEP)
    weight = weight - rate * (first_hat / (jnp.sqrt(second_hat) + ADAM_EPS) + WEIGHT_DECAY * weight)
    return (weight, first, second)


VMEM_BYTES = 48 * 1024 * 1024


def step_tiles(tile_count, col_count, offset=0):
    chunks = col_count // TS
    common = math.gcd(chunks, TS)
    group_tiles, group_rows = chunks // common, TS // common
    groups = tile_count // group_tiles
    best = 1
    for size in range(1, groups + 1):
        if groups % size or offset % (size * group_tiles) or (size * group_rows) % 16:
            continue
        best = size
        if size * group_tiles >= 24:
            break
    return best * group_tiles, best * group_rows


def fetch_matrix(sources, source_at, index_at, row_count, col_count):
    tile_count = row_count * col_count // (TS * TS)
    if col_count % TS:
        starts = np.cumsum([0] + [source.shape[0] for source in sources])
        index_at = index_at + jnp.array(starts[:-1], jnp.int32)[source_at]
        return jnp.concatenate(sources, axis=0)[index_at].reshape(row_count, col_count)
    chunks = col_count // TS
    tiles, rows = step_tiles(tile_count, col_count)
    steps = tile_count // tiles
    source_count = len(sources)

    def kernel(source_ref, index_ref, *refs):
        sources_in, out, land, wide, sems = refs[:source_count], *refs[source_count:]
        step = pl.program_id(0)

        def begin(which, slot):
            def one(tile, carry):
                at = which * tiles + tile
                source, index = source_ref[at], index_ref[at]

                def copy(low, high):
                    if high - low == 1:
                        pltpu.make_async_copy(
                            sources_in[low].at[index], land.at[slot, tile], sems.at[slot]
                        ).start()
                        return
                    middle = (low + high) // 2
                    pl.when(source < middle)(partial(copy, low, middle))
                    pl.when(source >= middle)(partial(copy, middle, high))

                copy(0, source_count)
                return carry

            lax.fori_loop(0, tiles, one, 0)

        @pl.when(step == 0)
        def _():
            begin(0, 0)

        @pl.when(step + 1 < steps)
        def _():
            begin(step + 1, lax.rem(step + 1, 2))

        slot = lax.rem(step, 2)
        pltpu.make_async_copy(land.at[slot], land.at[slot], sems.at[slot]).wait()
        wide[...] = land[slot].astype(jnp.float32).reshape(tiles * TS, TS)
        for chunk in range(chunks):
            out[:, chunk * TS : (chunk + 1) * TS] = wide[
                pl.ds(chunk, rows, stride=chunks), :
            ].astype(jnp.bfloat16)

    return pl.pallas_call(
        kernel,
        out_shape=jax.ShapeDtypeStruct((row_count, col_count), jnp.bfloat16),
        grid_spec=pltpu.PrefetchScalarGridSpec(
            num_scalar_prefetch=2,
            grid=(steps,),
            in_specs=[pl.BlockSpec(memory_space=pl.ANY)] * source_count,
            out_specs=pl.BlockSpec((rows, col_count), lambda i, *_: (i, 0)),
            scratch_shapes=[
                pltpu.VMEM((2, tiles, TS, TS), jnp.bfloat16),
                pltpu.VMEM((tiles * TS, TS), jnp.float32),
                pltpu.SemaphoreType.DMA((2,)),
            ],
        ),
        compiler_params=pltpu.CompilerParams(
            dimension_semantics=("arbitrary",), vmem_limit_bytes=VMEM_BYTES
        ),
        cost_estimate=pl.CostEstimate(
            flops=0, bytes_accessed=4 * row_count * col_count, transcendentals=0
        ),
        name="fetch_matrix",
    )(source_at, index_at, *sources)


def as_tiles(grad, into, offset):
    row_count, col_count = grad.shape
    grad = grad.astype(jnp.bfloat16)
    tile_count = row_count * col_count // (TS * TS)
    if col_count % TS:
        cut = grad.reshape(-1, TS, TS)
        if isinstance(into, int):
            into = jnp.zeros((into, TS, TS), jnp.bfloat16)
        return lax.dynamic_update_slice_in_dim(into, cut, offset, 0)
    chunks = col_count // TS
    tiles, rows = step_tiles(tile_count, col_count, offset)
    is_new = isinstance(into, int)

    def kernel(grad_ref, *refs):
        out, wide = refs[-2:]
        for chunk in range(chunks):
            wide[pl.ds(chunk, rows, stride=chunks), :] = grad_ref[
                :, chunk * TS : (chunk + 1) * TS
            ].astype(jnp.float32)
        out[...] = wide[...].reshape(tiles, TS, TS).astype(jnp.bfloat16)

    in_specs = [pl.BlockSpec((rows, col_count), lambda i: (i, 0))]
    return pl.pallas_call(
        kernel,
        out_shape=jax.ShapeDtypeStruct((into if is_new else into.shape[0], TS, TS), jnp.bfloat16),
        grid=(tile_count // tiles,),
        in_specs=in_specs if is_new else in_specs + [pl.BlockSpec(memory_space=pl.ANY)],
        out_specs=pl.BlockSpec((tiles, TS, TS), lambda i: (offset // tiles + i, 0, 0)),
        scratch_shapes=[pltpu.VMEM((tiles * TS, TS), jnp.float32)],
        input_output_aliases={} if is_new else {1: 0},
        compiler_params=pltpu.CompilerParams(
            dimension_semantics=("arbitrary",), vmem_limit_bytes=VMEM_BYTES
        ),
        cost_estimate=pl.CostEstimate(
            flops=0, bytes_accessed=4 * row_count * col_count, transcendentals=0
        ),
        name="as_tiles",
    )(*((grad,) if is_new else (grad, into)))


def ring_sizes(seq_count):
    return (4, seq_count // 8, 2)


def ring_send(block, sizes, dim):
    inner = math.prod(sizes[dim + 1 :])
    pairs = []
    for device in range(math.prod(sizes)):
        at = device // inner % sizes[dim]
        pairs.append((device, device + ((at + 1) % sizes[dim] - at) * inner))
    return lax.ppermute(block, "seq", pairs)


def nothing(*arrays):
    heads = [array.reshape(-1)[0] for array in arrays]
    return sum((head != head).astype(jnp.int32) for head in heads)


def sum_ticks(values, sizes):
    for dim, size in enumerate(sizes):
        moving = values
        for _ in range(size - 1):
            (moving,) = yield [ring_send(moving, sizes, dim)]
            values = values + moving
    return values


def added(left, right):
    return (left.astype(jnp.float32) + right.astype(jnp.float32)).astype(jnp.bfloat16)


def ring(parts, sizes, dim):
    moving = parts[1]
    for step in range(1, sizes[dim]):
        (came,) = yield [ring_send(moving, sizes, dim)]
        here = parts[(step + 1) % sizes[dim]]
        if step + 1 < sizes[dim]:
            moving = added(came, here)
    return came, here


def gather_ticks(block, sizes, order):
    parts = [block]
    for number, dim in enumerate(order):
        for _ in range(sizes[dim] - 1):
            parts += yield [ring_send(parts[-1], sizes, dim)]
        if number < 2:
            parts = [jnp.concatenate(parts, axis=0)]
    return parts


def scatter_ticks(terms, sizes, order):
    parts = [terms(step) for step in range(sizes[order[0]])]
    for number, dim in enumerate(order):
        came, here = yield from ring(parts, sizes, dim)
        if number < 2:
            parts = [added(came[at], here[at]) for at in range(sizes[order[number + 1]])]
    return added(came, here)


def together(*several):
    moving = [next(one) for one in several]
    results = [None] * len(several)
    while any(blocks is not None for blocks in moving):
        came = yield [block for blocks in moving if blocks is not None for block in blocks]
        for number, one in enumerate(several):
            if moving[number] is None:
                continue
            count = len(moving[number])
            mine, came = came[:count], came[count:]
            try:
                moving[number] = one.send(mine)
            except StopIteration as done:
                moving[number], results[number] = None, done.value
    return results


def gather_plane(block, sizes, order):
    parts = [block]
    for _ in range(sizes[order[0]] - 1):
        parts += yield [ring_send(parts[-1], sizes, order[0])]
    width = len(parts)
    for _ in range(sizes[order[1]] - 1):
        for part in parts[-width:]:
            parts = parts + (yield [ring_send(part, sizes, order[1])])
    return parts


def gather_pair(parts, width, sizes):
    while len(parts) < sizes[0]:
        parts += yield [ring_send(parts[-1], sizes, 0)]
    return (
        yield from together(
            gather_plane(jnp.concatenate([part[:width] for part in parts]), sizes, (1, 2)),
            gather_plane(jnp.concatenate([part[width:] for part in parts]), sizes, (2, 1)),
        )
    )


def scatter_plane(terms, sizes, order):
    first, second = order
    sums = [None] * sizes[second]
    for at in [*range(1, sizes[second]), 0]:
        sums[at] = added(
            *(yield from ring([terms(step, at) for step in range(sizes[first])], sizes, first))
        )
    return (yield from ring(sums, sizes, second))


def scatter_pair(terms, other_terms, sizes):
    left, right = yield from together(
        scatter_plane(terms, sizes, (2, 1)), scatter_plane(other_terms, sizes, (1, 2))
    )
    parts = [
        jnp.concatenate([added(came[at], here[at]) for came, here in (left, right)])
        for at in range(sizes[0])
    ]
    return added(*(yield from ring(parts, sizes, 0)))


class Ticks:
    def __init__(self):
        self.running = {}
        self.moving = {}
        self.results = {}

    def start(self, name, one):
        self.running[name] = one
        self.moving[name] = next(one)

    def tick(self, names, *others):
        names = [name for name in names if name in self.running]
        came = [self.moving[name] for name in names]
        if others:
            came, others = lax.optimization_barrier((came, others))
        for name, blocks in zip(names, came):
            try:
                self.moving[name] = self.running[name].send(blocks)
            except StopIteration as done:
                self.results[name] = done.value
                del self.running[name]
        return others[0] if len(others) == 1 else others

    def finish(self, names):
        while any(name in self.running for name in names):
            self.tick(names)
        return [self.results[name] for name in names]


GATHER_WIDE = (42, 34)


def portions(first, last, percent):
    wide = (percent * (last - first) + 50) // 100
    return first, min(first + wide, last), min(first + 2 * wide, last), last


def first_slots(tile_count, seq_count, capacity, percent):
    return min(capacity, -(-tile_count * percent // (100 * seq_count)))


def head_sum(partial_value):
    rounded = lax.optimization_barrier(partial_value.astype(jnp.bfloat16))
    if lax.axis_size("head") == 2:
        other = lax.ppermute(rounded, "head", [(0, 1), (1, 0)])
        return rounded.astype(jnp.float32) + other.astype(jnp.float32)
    return lax.psum(rounded, "head").astype(jnp.float32)


def adam_block(capacity):
    return max(size for size in (1, 2, 3, 4) if capacity % size == 0)


def first_pass_slot(cut_one, capacity):
    per = adam_block(capacity)
    return cut_one * 3 // 2 // per * per


def slot_cuts(seq_count, capacity, head_count, compact):
    shapes = piece_shapes(head_count)
    counts = [row_count * col_count // (TS * TS) for row_count, col_count in shapes]
    attn_tiles = sum(counts[:5])
    sent_tiles = sum(counts[:7])
    cut_one = first_slots(attn_tiles, seq_count, capacity, 126) if compact else capacity
    cut_two = first_slots(sent_tiles, seq_count, capacity, 112) if compact else capacity
    spare = (seq_count, 2 * seq_count) if compact else (0, 0)
    return attn_tiles, sent_tiles, cut_one, cut_two, spare


def layout_plan(owner_row, seq_count, capacity, head_count):
    attn_tiles, sent_tiles, cut_one, cut_two, spare = slot_cuts(
        seq_count, capacity, head_count, True
    )
    tile_count = owner_row.shape[0]
    tile_ids = jnp.arange(tile_count, dtype=jnp.int32)
    onehot = (owner_row[:, None] == jnp.arange(seq_count, dtype=jnp.int32)[None, :]).astype(
        jnp.int32
    )
    before = jnp.cumsum(onehot, axis=0) - onehot
    rank = jnp.sum(before * onehot, axis=1)
    is_attn = tile_ids < attn_tiles
    is_sent = tile_ids < sent_tiles
    over = [is_attn & (rank >= cut_one), is_sent & ~is_attn & (rank >= cut_two)]
    over_place = [jnp.cumsum(which.astype(jnp.int32)) - 1 for which in over]
    fits = (
        (jnp.sum(over[0].astype(jnp.int32)) <= spare[0])
        & (jnp.sum(over[1].astype(jnp.int32)) <= spare[1])
        & (jnp.max(jnp.where(is_attn, rank, 0)) < first_pass_slot(cut_one, capacity))
    )
    return (
        fits,
        rank,
        over[0] | over[1],
        jnp.where(over[0], over_place[0], spare[0] + over_place[1]),
    )


def listed_tiles(owner_row, rank, devices, cut):
    tile_ids = jnp.arange(owner_row.shape[0], dtype=jnp.float32)
    by_owner = (owner_row[None, :] == devices[:, None]).astype(jnp.float32)
    by_rank = (rank[:, None] == jnp.arange(cut, dtype=jnp.int32)[None, :]).astype(jnp.float32)
    return jnp.dot(by_owner * tile_ids[None, :], by_rank, precision=PRECISE).astype(jnp.int32)


def tile_factors(local, cond_ref, spread_ref, chunk_ref):
    conds, width = spread_ref.shape
    chunks = width // conds
    start = local * TS
    top = start // chunks
    place = start - top * chunks + lax.broadcasted_iota(jnp.int32, (TS, 1), 0)
    row_at = jnp.zeros((TS, 1), jnp.int32)
    for later in range(1, (TS + chunks - 2) // chunks + 1):
        row_at += (place >= later * chunks).astype(jnp.int32)
    chunk_at = place - row_at * chunks
    rows = 8 * ((TS + chunks - 2) // chunks // 8 + 1)
    picked = cond_ref[pl.ds(top, rows), :].astype(jnp.bfloat16)
    select = (row_at == lax.broadcasted_iota(jnp.int32, (TS, rows), 1)).astype(jnp.bfloat16)
    factor = jnp.dot(select, picked, preferred_element_type=jnp.float32).astype(jnp.bfloat16)
    wide = jnp.dot(factor, spread_ref[...], preferred_element_type=jnp.float32)
    return jnp.where(chunk_at == chunk_ref[...], wide, 0.0).astype(jnp.bfloat16)


def factor_tables(cond_rows, mod_cols):
    conds, chunks = cond_rows.shape[0], mod_cols // TS
    rows = 8 * ((TS + chunks - 2) // chunks // 8 + 1)
    columns = np.arange(conds * chunks)
    spread = (columns[None, :] % conds == np.arange(conds)[:, None]).astype(np.float32)
    return (
        jnp.pad(cond_rows.T.astype(jnp.float32), ((0, rows), (0, 0))),
        jnp.array(spread, jnp.bfloat16),
        jnp.array(columns[None, :] // conds, jnp.int32),
    )


def mod_product(tables, master, first_slot, slot_count, local):
    width = tables[1].shape[1]

    def kernel(meta_ref, local_ref, cond_ref, spread_ref, chunk_ref, master_ref, out, land, sems):
        first, count = meta_ref[0], meta_ref[1]

        def tile_copy(at):
            slot = lax.rem(at, 2)
            return pltpu.make_async_copy(master_ref.at[first + at], land.at[slot], sems.at[slot])

        out[...] = jnp.zeros_like(out)

        @pl.when(count > 0)
        def _():
            tile_copy(0).start()

        def one(at, carry):
            @pl.when(at + 1 < count)
            def _():
                tile_copy(at + 1).start()

            tile_copy(at).wait()
            factors = tile_factors(local_ref[first + at], cond_ref, spread_ref, chunk_ref)
            out[...] += lax.dot_general(
                factors,
                land[lax.rem(at, 2)].astype(jnp.bfloat16),
                (((0,), (0,)), ((), ())),
                preferred_element_type=jnp.float32,
            )
            return carry

        lax.fori_loop(0, count, one, 0)

    whole = pl.BlockSpec(memory_space=pltpu.VMEM)
    return pl.pallas_call(
        kernel,
        out_shape=jax.ShapeDtypeStruct((width, TS), jnp.float32),
        grid_spec=pltpu.PrefetchScalarGridSpec(
            num_scalar_prefetch=2,
            grid=(1,),
            in_specs=[whole, whole, whole, pl.BlockSpec(memory_space=pl.ANY)],
            out_specs=whole,
            scratch_shapes=[pltpu.VMEM((2, TS, TS), jnp.float32), pltpu.SemaphoreType.DMA((2,))],
        ),
        compiler_params=pltpu.CompilerParams(
            dimension_semantics=("arbitrary",), vmem_limit_bytes=VMEM_BYTES
        ),
        cost_estimate=pl.CostEstimate(
            flops=80 * width * TS * TS, bytes_accessed=40 * 4 * TS * TS, transcendentals=0
        ),
        name="mod_product",
    )(jnp.stack([first_slot, slot_count]), local, *tables, master)


def adam_slots(
    begin, end, into, tables, dmod, local, kind_of, over_at, rate, sums, over_sums, *state
):
    capacity = state[0].shape[0]
    per = adam_block(capacity)

    def kernel(*refs):
        local_ref, kind_ref, over_ref, rate_ref = refs[:4]
        cond_ref, spread_ref, chunk_ref, dmod_ref, over_sums_ref, sums_ref = refs[4:10]
        master_ref, first_ref, second_ref = refs[10:13]
        *outs, grad_ref = refs[-4:]
        step = pl.program_id(0) + begin // per
        for at in range(per):
            slot = step * per + at
            kind = kind_ref[slot]

            @pl.when(kind == 0)
            def _():
                grad_ref[...] = jnp.zeros_like(grad_ref)

            @pl.when(kind == 1)
            def _():
                grad_ref[...] = sums_ref[at].astype(jnp.float32)

            @pl.when(kind == 2)
            def _():
                grad_ref[...] = over_sums_ref[over_ref[slot]].astype(jnp.float32)

            @pl.when(kind == 3)
            def _():
                factors = tile_factors(local_ref[slot], cond_ref, spread_ref, chunk_ref)
                grad_ref[...] = jnp.dot(
                    factors, dmod_ref[...].astype(jnp.bfloat16), preferred_element_type=jnp.float32
                )

            results = adam_step(
                master_ref[at], first_ref[at], second_ref[at], grad_ref[...], rate_ref[slot]
            )
            for out, result in zip(outs, results):
                out[at] = result

    whole = pl.BlockSpec(memory_space=pltpu.VMEM)
    sums_block = pl.BlockSpec((per, TS, TS), lambda i, *_: (i, 0, 0))
    block = pl.BlockSpec((per, TS, TS), lambda i, *_: (i + begin // per, 0, 0))
    return pl.pallas_call(
        kernel,
        out_shape=[jax.ShapeDtypeStruct(state[0].shape, jnp.float32)] * 3,
        grid_spec=pltpu.PrefetchScalarGridSpec(
            num_scalar_prefetch=4,
            grid=((end - begin) // per,),
            in_specs=[whole] * 5
            + [sums_block]
            + [block] * 3
            + [pl.BlockSpec(memory_space=pl.ANY)] * len(into),
            out_specs=[block] * 3,
            scratch_shapes=[pltpu.VMEM((TS, TS), jnp.float32)],
        ),
        input_output_aliases={13 + number: number for number in range(len(into))},
        compiler_params=pltpu.CompilerParams(
            dimension_semantics=("arbitrary",), vmem_limit_bytes=VMEM_BYTES
        ),
        cost_estimate=pl.CostEstimate(
            flops=80 * spread_flops(tables),
            bytes_accessed=26 * (end - begin) * TS * TS,
            transcendentals=0,
        ),
        name="adam_slots",
    )(local, kind_of, over_at, rate, *tables, dmod, over_sums, sums, *state, *into)


def spread_flops(tables):
    return tables[1].shape[1] * TS * TS


def windowed(queries, keys, values, allowed, local_heads):
    micro_count, row_count = queries.shape[:2]
    query_heads = queries.reshape(micro_count, row_count, local_heads, HD)
    key_heads = keys.reshape(micro_count, -1, local_heads, HD)
    value_heads = values.reshape(micro_count, -1, local_heads, HD)
    scores = jnp.einsum(
        "mqhd,mkhd->mhqk", query_heads, key_heads, preferred_element_type=jnp.float32
    ) * HD ** (-0.5)
    scores = jnp.where(allowed[:, None], scores, MASKED)
    highest = jnp.max(scores, axis=-1, keepdims=True)
    expo = jnp.exp(scores - highest)
    total = jnp.sum(expo, axis=-1, keepdims=True)
    probs = (expo / total).astype(jnp.bfloat16)
    result = jnp.einsum("mhqk,mkhd->mqhd", probs, value_heads, preferred_element_type=jnp.float32)
    return (
        result.reshape(micro_count, row_count, -1).astype(jnp.bfloat16),
        highest + jnp.log(total),
    )


def windowed_back(queries, keys, values, allowed, log_total, grad_out, local_heads):
    micro_count, row_count = queries.shape[:2]
    scale = HD ** (-0.5)
    query_heads = queries.reshape(micro_count, row_count, local_heads, HD)
    key_heads = keys.reshape(micro_count, -1, local_heads, HD)
    value_heads = values.reshape(micro_count, -1, local_heads, HD)
    grad_heads = grad_out.reshape(micro_count, row_count, local_heads, HD)
    key_count = keys.shape[1]
    scores = (
        jnp.einsum("mqhd,mkhd->mhqk", query_heads, key_heads, preferred_element_type=jnp.float32)
        * scale
    )
    probs = jnp.where(allowed[:, None], jnp.exp(scores - log_total), 0.0)
    dprobs = jnp.einsum(
        "mqhd,mkhd->mhqk", grad_heads, value_heads, preferred_element_type=jnp.float32
    )
    dscores = (probs * (dprobs - jnp.sum(probs * dprobs, axis=-1, keepdims=True))).astype(
        jnp.bfloat16
    )
    dquery = (
        jnp.einsum("mhqk,mkhd->mqhd", dscores, key_heads, preferred_element_type=jnp.float32)
        * scale
    )
    dkey = (
        jnp.einsum("mhqk,mqhd->mkhd", dscores, query_heads, preferred_element_type=jnp.float32)
        * scale
    )
    dvalue = jnp.einsum(
        "mhqk,mqhd->mkhd",
        probs.astype(jnp.bfloat16),
        grad_heads,
        preferred_element_type=jnp.float32,
    )
    return (
        dquery.reshape(micro_count, row_count, -1),
        dkey.reshape(micro_count, key_count, -1),
        dvalue.reshape(micro_count, key_count, -1),
    )


def matmul(left, right):
    return jnp.dot(left, right, preferred_element_type=jnp.float32)


def one_step(
    compact,
    x_in,
    cotangent,
    cond,
    context,
    clip_lengths,
    pad_mask,
    owners,
    master,
    first_moment,
    second_moment,
    rank,
    over,
    over_place,
    second_step,
):
    seq_count = lax.axis_size("seq")
    head_count = lax.axis_size("head")
    me = lax.axis_index("seq")
    capacity = master.shape[1]
    micro_count, row_count = x_in.shape[:2]
    frames = pad_mask.shape[1]
    clip_count = clip_lengths.shape[1]
    head_cols = D // head_count
    ff_cols = FF // head_count
    mod_cols = 6 * D // head_count
    local_heads = head_cols // HD
    first_row = me * row_count
    token_count = micro_count * row_count
    clip_span = min(clip_count, row_count // MINLEN + 2)
    shapes = piece_shapes(head_count)

    owner_row = owners[0]
    cuts = slot_cuts(seq_count, capacity, head_count, compact)
    attn_tiles, sent_tiles, cut_one, cut_two, spare = cuts
    tile_ids = jnp.arange(owner_row.shape[0], dtype=jnp.int32)
    over_hit = over[None, :] & (
        over_place[None, :] == jnp.arange(sum(spare), dtype=jnp.int32)[:, None]
    )
    over_tile = jnp.sum(jnp.where(over_hit, tile_ids[None, :], 0), axis=1)
    over_mine = jnp.any(over_hit & (owner_row == me)[None, :], axis=1)
    slot_hit = (owner_row[None, :] == me) & (
        rank[None, :] == jnp.arange(capacity, dtype=jnp.int32)[:, None]
    )
    slot_used = jnp.any(slot_hit, axis=1)
    slot_tile = jnp.sum(jnp.where(slot_hit, tile_ids[None, :], 0), axis=1)
    slot_tile = jnp.where(slot_used, slot_tile, -1)

    own = master[0]
    sizes = ring_sizes(seq_count)
    offsets = [0]
    for row_total, col_total in shapes[:7]:
        offsets.append(offsets[-1] + row_total * col_total // (TS * TS))
    inner = [math.prod(sizes[dim + 1 :]) for dim in range(3)]
    back = [(me // inner[dim] - owner_row // inner[dim]) % sizes[dim] for dim in range(3)]
    over_rank = jnp.sum(jnp.where(over_hit, rank[None, :], 0), axis=1)
    steps_back = [
        (me // inner[dim] - jnp.arange(sizes[dim], dtype=jnp.int32)) % sizes[dim] * inner[dim]
        for dim in range(3)
    ]
    devices = (
        steps_back[0][:, None, None] + steps_back[1][None, :, None] + steps_back[2][None, None, :]
    ).reshape(-1)

    def by_home(listed):
        return listed.reshape(seq_count, -1)[devices].reshape(*sizes, -1)

    def home_of(place, each):
        device = place // each
        steps = [(me // inner[dim] - device // inner[dim]) % sizes[dim] for dim in range(3)]
        return steps, place - device * each

    ticks = Ticks()
    chunks = [(0, cut_one), (cut_one, cut_two)]
    gather_parts = [portions(*chunk, wide) for chunk, wide in zip(chunks, GATHER_WIDE)]
    scatter_parts = [portions(*chunk, 34) for chunk in chunks]
    if compact:

        def start_pair(number, *parts, shift=0.0):
            first, middle, second, _ = gather_parts[number]
            block = (own[first:second] + shift).astype(jnp.bfloat16)
            ticks.start(("pair", number), gather_pair([block, *parts], middle - first, sizes))

        def start_rest(number, *extra, shift=0.0):
            block = own[gather_parts[number][2] : gather_parts[number][3]]
            block = (block + shift).astype(jnp.bfloat16)
            block = jnp.concatenate([block, *extra], axis=0)
            ticks.start(("rest", number), gather_ticks(block, sizes, (2, 1, 0)))

        start_pair(0, second_step)
        over_low = jnp.where(
            by_home(over_mine)[..., None, None],
            own[by_home(over_rank)].astype(jnp.bfloat16),
            jnp.zeros((), jnp.bfloat16),
        ).transpose(2, 1, 0, 3, 4, 5)
        ticks.start("over", scatter_ticks(lambda step: over_low[step], sizes, (2, 1, 0)))
        start_rest(0, ticks.finish(["over"])[0])
        for _ in range(sizes[0] - 2):
            ticks.tick([("pair", 0)])
        on_plane = ticks.moving["pair", 0]
        ticks.tick([("pair", 0)])
        start_pair(1, shift=nothing(*on_plane).astype(jnp.float32))
        on_plane = ticks.moving["pair", 0]
        ticks.finish([("pair", 0), ("rest", 0)])
        start_rest(1, shift=nothing(*on_plane).astype(jnp.float32))

    cond_rows = cond.reshape(micro_count * clip_count, D)
    tables = factor_tables(cond_rows, mod_cols)
    local = jnp.maximum(slot_tile - sent_tiles, 0)
    is_mod = slot_tile >= sent_tiles
    mod_count = jnp.sum(is_mod.astype(jnp.int32))
    tiles_here = jnp.sum((owner_row == me).astype(jnp.int32))
    mod_part = mod_product(tables, own, tiles_here - mod_count, mod_count, local)
    mod_part = (
        mod_part.reshape(mod_cols // TS, micro_count * clip_count, TS)
        .transpose(1, 0, 2)
        .reshape(micro_count * clip_count, mod_cols)
    )
    mod_all = lax.all_gather(lax.psum(mod_part, "seq"), "head", axis=1, tiled=True)

    weights = {}

    def fetch(kinds, numbers):
        if compact:
            each = sum(spare) // seq_count
            pools, source_at, index_at = [], jnp.zeros_like(rank), jnp.zeros_like(rank)
            steps, at = home_of(over_place, each)
            for number in numbers:
                first, middle, second, last = gather_parts[number]
                extra = 0 if number else each
                here = ~over & (rank >= second) & (rank < last)
                slot, block = rank - second, back
                if not number:
                    here = here | over
                    slot = jnp.where(over, last - second + at, slot)
                    block = [jnp.where(over, steps[dim], back[dim]) for dim in range(3)]
                source_at = jnp.where(here, len(pools) + block[0], source_at)
                index_at = jnp.where(
                    here, (block[1] * sizes[2] + block[2]) * (last - second + extra) + slot, index_at
                )
                pools = pools + ticks.results["rest", number]
                for which, (low, high, one, two) in enumerate(
                    [(first, middle, 2, 1), (middle, second, 1, 2)]
                ):
                    here = ~over & (rank >= low) & (rank < high)
                    array_at = back[one] * sizes[two] + back[two]
                    source_at = jnp.where(here, len(pools) + array_at, source_at)
                    index_at = jnp.where(here, back[0] * (high - low) + rank - low, index_at)
                    pools = pools + ticks.results["pair", number][which]
        else:
            pools = [lax.all_gather(own.astype(jnp.bfloat16), "seq", axis=0, tiled=True)]
            source_at = jnp.zeros_like(rank)
            index_at = owner_row * capacity + rank
        for kind in kinds:
            begin, end = offsets[kind : kind + 2]
            weights[kind] = fetch_matrix(
                pools, source_at[begin:end], index_at[begin:end], *shapes[kind]
            )

    if compact:
        fetch(range(5), [0])
    else:
        fetch(range(7), None)
    w_qkv, w_out, w_cq, w_ckv, w_cout = [weights[kind] for kind in range(5)]

    positions = first_row + jnp.arange(row_count, dtype=jnp.int32)
    ext_pos = first_row - WIN + jnp.arange(row_count + 2 * WIN, dtype=jnp.int32)
    near_keys, clip_keys, onehots, ctx_rows = [], [], [], []
    for micro_idx in range(micro_count):
        lengths = clip_lengths[micro_idx]
        clip_tok = clip_ids(lengths, positions)
        clip_start = jnp.minimum(clip_tok[0], clip_count - clip_span)
        key_clip = clip_start + jnp.arange(clip_span * CTX, dtype=jnp.int32) // CTX
        mask_pad = jnp.pad(pad_mask[micro_idx], (WIN, WIN))
        ext_flag = lax.dynamic_slice_in_dim(mask_pad, first_row, row_count + 2 * WIN, 0)
        near_keys.append(window_mask(positions, ext_pos, ext_flag, lengths, frames))
        clip_keys.append(clip_tok[:, None] == key_clip[None, :])
        listed = micro_idx * clip_count + clip_tok
        onehots.append(
            listed[:, None] == jnp.arange(micro_count * clip_count, dtype=jnp.int32)[None, :]
        )
        ctx_rows.append(
            lax.dynamic_slice_in_dim(context[micro_idx], clip_start, clip_span, 0).reshape(
                clip_span * CTX, DC
            )
        )
    near_keys, clip_keys = jnp.stack(near_keys), jnp.stack(clip_keys)
    onehot = jnp.concatenate(onehots, axis=0).astype(jnp.float32)
    ctx_rows = jnp.concatenate(ctx_rows, axis=0)

    def by_micro(rows):
        return rows.reshape(micro_count, -1, rows.shape[-1])

    def flat(rows):
        return rows.reshape(-1, rows.shape[-1])

    mod_frames = jnp.dot(onehot, mod_all, precision=PRECISE)
    shifts = [mod_frames[:, 2 * which * D : (2 * which + 1) * D] for which in range(3)]
    scales = [mod_frames[:, (2 * which + 1) * D : (2 * which + 2) * D] for which in range(3)]
    resid_zero = flat(x_in).astype(jnp.float32)
    normed_one, inverse_one = layer_norm(resid_zero)
    input_one = (normed_one * (1.0 + scales[0]) + shifts[0]).astype(jnp.bfloat16)
    proj_qkv = by_micro(matmul(input_one, w_qkv).astype(jnp.bfloat16))
    queries = proj_qkv[:, :, :head_cols]
    kv_ext = padded(proj_qkv[:, :, head_cols:], (("seq", 1),), WIN)
    attended, log_one = windowed(
        queries, kv_ext[:, :, :head_cols], kv_ext[:, :, head_cols:], near_keys, local_heads
    )
    resid_one = resid_zero + head_sum(matmul(flat(attended), w_out))
    normed_two, inverse_two = layer_norm(resid_one)
    input_two = (normed_two * (1.0 + scales[1]) + shifts[1]).astype(jnp.bfloat16)
    cross_query = by_micro(matmul(input_two, w_cq).astype(jnp.bfloat16))
    cross_kv = by_micro(matmul(ctx_rows, w_ckv).astype(jnp.bfloat16))
    cross_out, log_two = windowed(
        cross_query, cross_kv[:, :, :head_cols], cross_kv[:, :, head_cols:], clip_keys, local_heads
    )
    resid_two = resid_one + head_sum(matmul(flat(cross_out), w_cout))
    if compact:
        ticks.finish([("pair", 1), ("rest", 1)])
        fetch((6, 5), [0, 1])
    w_glu, w_down = weights[5], weights[6]
    normed_three, inverse_three = layer_norm(resid_two)
    input_three = (normed_three * (1.0 + scales[2]) + shifts[2]).astype(jnp.bfloat16)
    gate_up = matmul(input_three, w_glu)
    gate_part = gate_up[:, :ff_cols]
    up_part = gate_up[:, ff_cols:]
    sigmoid_gate = jax.nn.sigmoid(gate_part)
    silu_gate = gate_part * sigmoid_gate
    hidden = (silu_gate * up_part).astype(jnp.bfloat16)

    grad_low = flat(cotangent)
    grad_three = grad_low.astype(jnp.float32)
    pool_ff = as_tiles(matmul(hidden.T, grad_low), sent_tiles, offsets[6])
    grad_hidden = matmul(grad_low, w_down.T)
    dglu = jnp.concatenate(
        [
            grad_hidden * up_part * sigmoid_gate * (1.0 + gate_part * (1.0 - sigmoid_gate)),
            grad_hidden * silu_gate,
        ],
        axis=1,
    ).astype(jnp.bfloat16)
    pool_ff = as_tiles(matmul(input_three.T, dglu), pool_ff, offsets[5])
    slots = listed_tiles(owner_row, rank, devices, cut_two)

    def start_scatter(number, pool, listed, gate=()):
        first, middle, second, last = scatter_parts[number]
        wanted = jnp.concatenate(
            [slots.reshape(*sizes, cut_two), by_home(listed)], axis=3
        )
        if number:
            wanted = jnp.maximum(wanted, attn_tiles)
        taken = []

        def pick(places, *before):
            return pool[places + nothing(*before)]


        def plane(low, high, order):
            here = wanted[..., low:high].transpose(*order, 0, 3)
            sent = [
                [pick(here[step, at], *gate) for at in range(sizes[order[1]])]
                for step in range(1, sizes[order[0]])
            ]
            kept = pick(here[0], *(() if gate else sum(sent, [])))
            taken.extend([*sum(sent, []), kept])
            return lambda step, at: sent[step - 1][at] if step else kept[at]

        one, two = plane(first, middle, (2, 1)), plane(middle, second, (1, 2))
        here = jnp.concatenate([wanted[..., second:last], wanted[..., cut_two:]], axis=3)
        sent = pick(here[1], *gate)
        kept = pick(jnp.concatenate([here[:1], here[2:]]), *(() if gate else (sent,)))
        taken.extend([sent, kept])
        ticks.start(("pair", number), scatter_pair(one, two, sizes))
        ticks.start(
            ("rest", number),
            scatter_ticks(
                lambda step: sent if step == 1 else kept[max(step - 1, 0)], sizes, (0, 1, 2)
            ),
        )
        return taken

    def start_out(number):
        total = ticks.finish([("rest", number)])[0]
        total = total[scatter_parts[number][3] - scatter_parts[number][2] :]
        ticks.start(("out", number), gather_ticks(total, sizes, (0, 1, 2)))

    if compact:
        taken = start_scatter(1, pool_ff, over_tile[spare[0] :])
        pool_ff, _ = lax.optimization_barrier((pool_ff, taken))
    back_three, dscale_three, dshift_three = norm_back(
        head_sum(matmul(dglu, w_glu.T)), normed_three, inverse_three, scales[2]
    )
    grad_two = grad_three + back_three
    grad_low = grad_two.astype(jnp.bfloat16)
    grad_cout = matmul(flat(cross_out).T, grad_low).astype(jnp.bfloat16)
    grad_cross = by_micro(matmul(grad_low, w_cout.T).astype(jnp.bfloat16))
    dquery_two, dkey_two, dvalue_two = windowed_back(
        cross_query,
        cross_kv[:, :, :head_cols],
        cross_kv[:, :, head_cols:],
        clip_keys,
        log_two,
        grad_cross,
        local_heads,
    )
    dquery_two = flat(dquery_two).astype(jnp.bfloat16)
    pool = as_tiles(grad_cout, pool_ff, offsets[4])
    pool = as_tiles(matmul(input_two.T, dquery_two), pool, offsets[2])
    dkv_two = flat(jnp.concatenate([dkey_two, dvalue_two], axis=2)).astype(jnp.bfloat16)
    pool = as_tiles(matmul(ctx_rows.T, dkv_two), pool, offsets[3])
    back_two, dscale_two, dshift_two = norm_back(
        head_sum(matmul(dquery_two, w_cq.T)), normed_two, inverse_two, scales[1]
    )
    grad_one = grad_two + back_two
    grad_low = grad_one.astype(jnp.bfloat16)
    pool = as_tiles(matmul(flat(attended).T, grad_low), pool, offsets[1])
    grad_attended = by_micro(matmul(grad_low, w_out.T).astype(jnp.bfloat16))
    dquery_one, dkey_ext, dvalue_ext = windowed_back(
        queries,
        kv_ext[:, :, :head_cols],
        kv_ext[:, :, head_cols:],
        near_keys,
        log_one,
        grad_attended,
        local_heads,
    )
    dkv_ext = jnp.concatenate([dkey_ext, dvalue_ext], axis=2)
    rims = jnp.concatenate([dkv_ext[:, :WIN], dkv_ext[:, row_count + WIN :]], axis=1)
    returned = padded(rims.astype(jnp.bfloat16), (("seq", 1),), WIN).astype(jnp.float32)
    dkv_own = dkv_ext[:, WIN : row_count + WIN]
    dkv_own = dkv_own.at[:, :WIN].add(returned[:, :WIN])
    dkv_own = dkv_own.at[:, row_count - WIN :].add(returned[:, 3 * WIN :])
    dqkv = flat(jnp.concatenate([dquery_one, dkv_own], axis=2).astype(jnp.bfloat16))
    pool = as_tiles(matmul(input_one.T, dqkv), pool, offsets[0])
    back_one, dscale_one, dshift_one = norm_back(
        head_sum(matmul(dqkv, w_qkv.T)), normed_one, inverse_one, scales[0]
    )
    grad_input = by_micro(grad_one + back_one)

    dmod = jnp.concatenate(
        [
            jnp.dot(onehot.T, rows, precision=PRECISE)
            for rows in (
                dshift_one,
                dscale_one,
                dshift_two,
                dscale_two,
                dshift_three,
                dscale_three,
            )
        ],
        axis=1,
    )
    dmod = lax.dynamic_slice_in_dim(dmod, lax.axis_index("head") * mod_cols, mod_cols, 1)
    ticks.start("dmod", sum_ticks(dmod, sizes))
    (dmod,) = ticks.finish(["dmod"])
    gate = [dmod]
    if compact:
        gate = start_scatter(0, pool, over_tile[: spare[0]], [dmod])
        start_out(1)
        ticks.finish([("out", 1)])
    late = (hidden.astype(jnp.float32) + nothing(gate[0]).astype(jnp.float32)).astype(jnp.bfloat16)
    out_block = by_micro((resid_two + head_sum(matmul(late, w_down))).astype(jnp.bfloat16))
    dmod = (
        dmod
        .reshape(micro_count * clip_count, mod_cols // TS, TS)
        .transpose(1, 0, 2)
        .reshape(-1, TS)
    )

    state = (own, first_moment[0], second_moment[0])
    rate = slot_rates(slot_tile, shapes)
    if compact:
        over_slot = slot_hit & over[None, :]
        slot_over = jnp.any(over_slot, axis=1)
        over_at = jnp.sum(jnp.where(over_slot, over_place[None, :], 0), axis=1)
        kind_of = jnp.where(is_mod, 3, jnp.where(slot_over, 2, slot_used.astype(jnp.int32)))
        slot = first_pass_slot(cut_one, capacity)

        def sums_of(number):
            first, _, second, last = scatter_parts[number]
            pair, rest = ticks.finish([("pair", number), ("rest", number)])
            return [pair, rest[: last - second]]

        def over_sums_of(number):
            each = spare[number] // seq_count
            place = over_at - (spare[0] if number else 0)
            steps, at = home_of(place, each)
            block = (steps[2] * sizes[1] + steps[1]) * sizes[0] + steps[0]
            (sums,) = ticks.finish([("out", number)])
            return jnp.concatenate(sums, axis=0), block * each + at

        later = jnp.concatenate(
            [*sums_of(1), jnp.zeros((capacity - cut_two, TS, TS), jnp.bfloat16)], axis=0
        )
        over_sums, over_index = over_sums_of(1)
        results = adam_slots(
            slot,
            capacity,
            (),
            tables,
            dmod,
            local,
            kind_of,
            jnp.clip(over_index, 0, over_sums.shape[0] - 1),
            rate,
            later[slot - cut_one :],
            over_sums,
            *state,
        )
        ticks.finish([("rest", 0)])
        start_out(0)
        sooner = jnp.concatenate([*sums_of(0), later[: slot - cut_one]], axis=0)
        over_sums, over_index = over_sums_of(0)
        results = adam_slots(
            0,
            slot,
            results,
            tables,
            dmod,
            local,
            kind_of,
            jnp.clip(over_index, 0, over_sums.shape[0] - 1),
            rate,
            sooner,
            over_sums,
            *state,
        )
    else:
        sums = lax.psum_scatter(
            pool[listed_tiles(owner_row, rank, jnp.arange(seq_count), capacity).reshape(-1)],
            "seq",
            scatter_dimension=0,
            tiled=True,
        )
        results = adam_slots(
            0,
            capacity,
            (),
            tables,
            dmod,
            local,
            jnp.where(is_mod, 3, slot_used.astype(jnp.int32)),
            jnp.zeros_like(slot_tile),
            rate,
            sums,
            jnp.zeros((1, TS, TS), jnp.bfloat16),
            *state,
        )
    weight, first, second = results
    return (out_block, grad_input, weight[None], first[None], second[None])


def on_device(*args):
    owner_row, own = args[6][0], args[7][0]
    seq_count, capacity = lax.axis_size("seq"), own.shape[0]
    head_count = lax.axis_size("head")
    first, _, second, _ = portions(
        0, slot_cuts(seq_count, capacity, head_count, True)[2], GATHER_WIDE[0]
    )
    block = own[first:second].astype(jnp.bfloat16)
    second_step = ring_send(block, ring_sizes(seq_count), 0)
    fits, *plan = layout_plan(owner_row, seq_count, capacity, head_count)
    misfits = lax.pmax(1 - fits.astype(jnp.int32), "head")
    return lax.cond(
        misfits == 0, partial(one_step, True), partial(one_step, False), *args, *plan, second_step
    )


def solution(mesh):
    placed = (
        P(None, "seq", None),
        P(None, "seq", None),
        P(),
        P(),
        P(),
        P(),
        P("head", None),
        P("head", "seq", None, None),
        P("head", "seq", None, None),
        P("head", "seq", None, None),
    )
    return jax.shard_map(
        on_device,
        mesh=mesh,
        in_specs=placed,
        out_specs=(
            P(None, "seq", None),
            P(None, "seq", None),
            P("head", "seq", None, None),
            P("head", "seq", None, None),
            P("head", "seq", None, None),
        ),
        check_vma=False,
    )
```

```python
import math
from functools import partial

import jax
import jax.numpy as jnp
import numpy as np
from jax import lax
from jax.experimental import pallas as pl
from jax.experimental.pallas import tpu as pltpu
from jax.sharding import PartitionSpec as P

D = 1536
HD = 64
FF = 6144
DC = 768
CTX = 128
WIN = 128
TS = 128
STEP = 5
MINLEN = 204


PRECISE = lax.Precision.HIGHEST
EPS_NORM = 1e-06
BETA_ONE = 0.9
BETA_TWO = 0.95
ADAM_EPS = 1e-08
WEIGHT_DECAY = 0.1
LEARN_RATE = 0.5
MASKED = -1e30


def padded(shard, sides, width):
    for axis, dim in sides:
        size, length = (lax.axis_size(axis), shard.shape[dim])
        up = [(i, (i + 1) % size) for i in range(size - 1)]
        down = [(j, i) for i, j in up]
        last = lax.slice_in_dim(shard, length - width, length, axis=dim)
        initial = lax.slice_in_dim(shard, 0, width, axis=dim)
        before = lax.ppermute(last, axis, up)
        after = lax.ppermute(initial, axis, down)
        shard = jnp.concatenate([before, shard, after], axis=dim)
    return shard


def piece_shapes(head_count):
    head_cols = D // head_count
    ff_cols = FF // head_count
    return [
        (D, 3 * head_cols),
        (head_cols, D),
        (D, head_cols),
        (DC, 2 * head_cols),
        (head_cols, D),
        (D, 2 * ff_cols),
        (ff_cols, D),
        (D, 6 * D // head_count),
    ]


def fan_inputs():
    return [D, D // 64, D, DC, D // 32, D, FF // 4, 4 * D]


def slot_rates(slot_tile, shapes):
    counts = [row_count * col_count // (TS * TS) for row_count, col_count in shapes]
    kind_ends = jnp.array([int(end_value) for end_value in np.cumsum(counts)[:-1]], dtype=jnp.int32)
    slot_kind = jnp.sum((slot_tile[:, None] >= kind_ends[None, :]).astype(jnp.int32), axis=1)
    rate_table = jnp.array(
        [LEARN_RATE * fan_in ** (-0.5) for fan_in in fan_inputs()], dtype=jnp.float32
    )
    onehot = (slot_kind[:, None] == jnp.arange(len(shapes), dtype=jnp.int32)[None, :]).astype(
        jnp.float32
    )
    return jnp.sum(onehot * rate_table[None, :], axis=1)


def split_pieces(flattened, shapes):
    pieces = []
    offset = 0
    for row_count, col_count in shapes:
        pieces.append(
            flattened[offset : offset + row_count * col_count].reshape(row_count, col_count)
        )
        offset = offset + row_count * col_count
    return pieces


def layer_norm(values):
    centred = values - jnp.mean(values, axis=-1, keepdims=True)
    inverse = lax.rsqrt(jnp.mean(centred * centred, axis=-1, keepdims=True) + EPS_NORM)
    return (centred * inverse, inverse)


def norm_back(grad, normed, inverse, scale_part):
    dnormed = grad * (1.0 + scale_part)
    dvalues = inverse * (
        dnormed
        - jnp.mean(dnormed, axis=-1, keepdims=True)
        - normed * jnp.mean(dnormed * normed, axis=-1, keepdims=True)
    )
    return (dvalues, grad * normed, grad)


def clip_ids(lengths, positions):
    clip_ends = jnp.cumsum(lengths)
    return jnp.sum((positions[:, None] >= clip_ends[None, :]).astype(jnp.int32), axis=1)


def window_mask(query_pos, key_pos, key_flag, lengths, frames):
    query_clip = clip_ids(lengths, query_pos)
    key_clip = clip_ids(lengths, key_pos)
    offset = key_pos[None, :] - query_pos[:, None]
    is_near = (offset <= WIN) & (offset >= -WIN)
    is_inside = (key_pos >= 0) & (key_pos < frames)
    same_clip = query_clip[:, None] == key_clip[None, :]
    is_kept = (key_flag[None, :] == 1) | (offset == 0)
    return is_near & is_inside[None, :] & same_clip & is_kept


def adam_step(weight, first, second, grads, rate):
    first = BETA_ONE * first + (1.0 - BETA_ONE) * grads
    second = BETA_TWO * second + (1.0 - BETA_TWO) * grads * grads
    first_hat = first / (1.0 - BETA_ONE**STEP)
    second_hat = second / (1.0 - BETA_TWO**STEP)
    weight = weight - rate * (first_hat / (jnp.sqrt(second_hat) + ADAM_EPS) + WEIGHT_DECAY * weight)
    return (weight, first, second)


VMEM_BYTES = 48 * 1024 * 1024


def step_tiles(tile_count, col_count, offset=0):
    chunks = col_count // TS
    common = math.gcd(chunks, TS)
    group_tiles, group_rows = chunks // common, TS // common
    groups = tile_count // group_tiles
    best = 1
    for size in range(1, groups + 1):
        if groups % size or offset % (size * group_tiles) or (size * group_rows) % 16:
            continue
        best = size
        if size * group_tiles >= 24:
            break
    return best * group_tiles, best * group_rows


def fetch_matrix(sources, source_at, index_at, row_count, col_count):
    tile_count = row_count * col_count // (TS * TS)
    if col_count % TS:
        starts = np.cumsum([0] + [source.shape[0] for source in sources])
        index_at = index_at + jnp.array(starts[:-1], jnp.int32)[source_at]
        return jnp.concatenate(sources, axis=0)[index_at].reshape(row_count, col_count)
    chunks = col_count // TS
    tiles, rows = step_tiles(tile_count, col_count)
    steps = tile_count // tiles
    source_count = len(sources)

    def kernel(source_ref, index_ref, *refs):
        sources_in, out, land, wide, sems = refs[:source_count], *refs[source_count:]
        step = pl.program_id(0)

        def begin(which, slot):
            def one(tile, carry):
                at = which * tiles + tile
                source, index = source_ref[at], index_ref[at]

                def copy(low, high):
                    if high - low == 1:
                        pltpu.make_async_copy(
                            sources_in[low].at[index], land.at[slot, tile], sems.at[slot]
                        ).start()
                        return
                    middle = (low + high) // 2
                    pl.when(source < middle)(partial(copy, low, middle))
                    pl.when(source >= middle)(partial(copy, middle, high))

                copy(0, source_count)
                return carry

            lax.fori_loop(0, tiles, one, 0)

        @pl.when(step == 0)
        def _():
            begin(0, 0)

        @pl.when(step + 1 < steps)
        def _():
            begin(step + 1, lax.rem(step + 1, 2))

        slot = lax.rem(step, 2)
        pltpu.make_async_copy(land.at[slot], land.at[slot], sems.at[slot]).wait()
        wide[...] = land[slot].astype(jnp.float32).reshape(tiles * TS, TS)
        for chunk in range(chunks):
            out[:, chunk * TS : (chunk + 1) * TS] = wide[
                pl.ds(chunk, rows, stride=chunks), :
            ].astype(jnp.bfloat16)

    return pl.pallas_call(
        kernel,
        out_shape=jax.ShapeDtypeStruct((row_count, col_count), jnp.bfloat16),
        grid_spec=pltpu.PrefetchScalarGridSpec(
            num_scalar_prefetch=2,
            grid=(steps,),
            in_specs=[pl.BlockSpec(memory_space=pl.ANY)] * source_count,
            out_specs=pl.BlockSpec((rows, col_count), lambda i, *_: (i, 0)),
            scratch_shapes=[
                pltpu.VMEM((2, tiles, TS, TS), jnp.bfloat16),
                pltpu.VMEM((tiles * TS, TS), jnp.float32),
                pltpu.SemaphoreType.DMA((2,)),
            ],
        ),
        compiler_params=pltpu.CompilerParams(
            dimension_semantics=("arbitrary",), vmem_limit_bytes=VMEM_BYTES
        ),
        cost_estimate=pl.CostEstimate(
            flops=0, bytes_accessed=4 * row_count * col_count, transcendentals=0
        ),
        name="fetch_matrix",
    )(source_at, index_at, *sources)


def as_tiles(grad, into, offset):
    row_count, col_count = grad.shape
    grad = grad.astype(jnp.bfloat16)
    tile_count = row_count * col_count // (TS * TS)
    if col_count % TS:
        cut = grad.reshape(-1, TS, TS)
        if isinstance(into, int):
            into = jnp.zeros((into, TS, TS), jnp.bfloat16)
        return lax.dynamic_update_slice_in_dim(into, cut, offset, 0)
    chunks = col_count // TS
    tiles, rows = step_tiles(tile_count, col_count, offset)
    is_new = isinstance(into, int)

    def kernel(grad_ref, *refs):
        out, wide = refs[-2:]
        for chunk in range(chunks):
            wide[pl.ds(chunk, rows, stride=chunks), :] = grad_ref[
                :, chunk * TS : (chunk + 1) * TS
            ].astype(jnp.float32)
        out[...] = wide[...].reshape(tiles, TS, TS).astype(jnp.bfloat16)

    in_specs = [pl.BlockSpec((rows, col_count), lambda i: (i, 0))]
    return pl.pallas_call(
        kernel,
        out_shape=jax.ShapeDtypeStruct((into if is_new else into.shape[0], TS, TS), jnp.bfloat16),
        grid=(tile_count // tiles,),
        in_specs=in_specs if is_new else in_specs + [pl.BlockSpec(memory_space=pl.ANY)],
        out_specs=pl.BlockSpec((tiles, TS, TS), lambda i: (offset // tiles + i, 0, 0)),
        scratch_shapes=[pltpu.VMEM((tiles * TS, TS), jnp.float32)],
        input_output_aliases={} if is_new else {1: 0},
        compiler_params=pltpu.CompilerParams(
            dimension_semantics=("arbitrary",), vmem_limit_bytes=VMEM_BYTES
        ),
        cost_estimate=pl.CostEstimate(
            flops=0, bytes_accessed=4 * row_count * col_count, transcendentals=0
        ),
        name="as_tiles",
    )(*((grad,) if is_new else (grad, into)))


def ring_sizes(seq_count):
    return (4, seq_count // 8, 2)


def ring_send(block, sizes, dim):
    inner = math.prod(sizes[dim + 1 :])
    pairs = []
    for device in range(math.prod(sizes)):
        at = device // inner % sizes[dim]
        pairs.append((device, device + ((at + 1) % sizes[dim] - at) * inner))
    return lax.ppermute(block, "seq", pairs)


def nothing(*arrays):
    heads = [array.reshape(-1)[0] for array in arrays]
    return sum((head != head).astype(jnp.int32) for head in heads)


def sum_ticks(values, sizes):
    for dim, size in enumerate(sizes):
        moving = values
        for _ in range(size - 1):
            (moving,) = yield [ring_send(moving, sizes, dim)]
            values = values + moving
    return values


def added(left, right):
    return (left.astype(jnp.float32) + right.astype(jnp.float32)).astype(jnp.bfloat16)


def ring(parts, sizes, dim):
    moving = parts[1]
    for step in range(1, sizes[dim]):
        (came,) = yield [ring_send(moving, sizes, dim)]
        here = parts[(step + 1) % sizes[dim]]
        if step + 1 < sizes[dim]:
            moving = added(came, here)
    return came, here


def gather_ticks(block, sizes, order):
    parts = [block]
    for number, dim in enumerate(order):
        for _ in range(sizes[dim] - 1):
            parts += yield [ring_send(parts[-1], sizes, dim)]
        if number < 2:
            parts = [jnp.concatenate(parts, axis=0)]
    return parts


def scatter_ticks(terms, sizes, order):
    parts = [terms(step) for step in range(sizes[order[0]])]
    for number, dim in enumerate(order):
        came, here = yield from ring(parts, sizes, dim)
        if number < 2:
            parts = [added(came[at], here[at]) for at in range(sizes[order[number + 1]])]
    return added(came, here)


def together(*several):
    moving = [next(one) for one in several]
    results = [None] * len(several)
    while any(blocks is not None for blocks in moving):
        came = yield [block for blocks in moving if blocks is not None for block in blocks]
        for number, one in enumerate(several):
            if moving[number] is None:
                continue
            count = len(moving[number])
            mine, came = came[:count], came[count:]
            try:
                moving[number] = one.send(mine)
            except StopIteration as done:
                moving[number], results[number] = None, done.value
    return results


def gather_plane(block, sizes, order):
    parts = [block]
    for _ in range(sizes[order[0]] - 1):
        parts += yield [ring_send(parts[-1], sizes, order[0])]
    width = len(parts)
    for _ in range(sizes[order[1]] - 1):
        for part in parts[-width:]:
            parts = parts + (yield [ring_send(part, sizes, order[1])])
    return parts


def gather_pair(parts, width, sizes):
    while len(parts) < sizes[0]:
        parts += yield [ring_send(parts[-1], sizes, 0)]
    return (
        yield from together(
            gather_plane(jnp.concatenate([part[:width] for part in parts]), sizes, (1, 2)),
            gather_plane(jnp.concatenate([part[width:] for part in parts]), sizes, (2, 1)),
        )
    )


def scatter_plane(parts, sizes, order):
    first, second = order
    came, here = yield from ring(parts, sizes, first)
    sums = [added(came[at], here[at]) for at in range(sizes[second])]
    return (yield from ring(sums, sizes, second))


def scatter_pair(terms, other_terms, sizes):
    left, right = yield from together(
        scatter_plane(terms, sizes, (2, 1)), scatter_plane(other_terms, sizes, (1, 2))
    )
    parts = [
        jnp.concatenate([added(came[at], here[at]) for came, here in (left, right)])
        for at in range(sizes[0])
    ]
    return added(*(yield from ring(parts, sizes, 0)))


class Ticks:
    def __init__(self):
        self.running = {}
        self.moving = {}
        self.results = {}

    def start(self, name, one):
        self.running[name] = one
        self.moving[name] = next(one)

    def tick(self, names, value=None):
        names = [name for name in names if name in self.running]
        came = [self.moving[name] for name in names]
        if value is not None and names:
            value = value + nothing(*sum(came, [])).astype(value.dtype)
        for name, blocks in zip(names, came):
            try:
                self.moving[name] = self.running[name].send(blocks)
            except StopIteration as done:
                self.results[name] = done.value
                del self.running[name]
        return value

    def finish(self, names):
        while any(name in self.running for name in names):
            self.tick(names)
        return [self.results[name] for name in names]


GATHER_WIDE = (42, 34)


def portions(first, last, percent):
    wide = (percent * (last - first) + 50) // 100
    return first, min(first + wide, last), min(first + 2 * wide, last), last


def first_slots(tile_count, seq_count, capacity, percent):
    return min(capacity, -(-tile_count * percent // (100 * seq_count)))


def head_sum(partial_value):
    rounded = lax.optimization_barrier(partial_value.astype(jnp.bfloat16))
    if lax.axis_size("head") == 2:
        other = lax.ppermute(rounded, "head", [(0, 1), (1, 0)])
        return rounded.astype(jnp.float32) + other.astype(jnp.float32)
    return lax.psum(rounded, "head").astype(jnp.float32)


def adam_block(capacity):
    return max(size for size in (1, 2, 3, 4) if capacity % size == 0)


def first_pass_slot(cut_one, capacity):
    per = adam_block(capacity)
    return cut_one * 3 // 2 // per * per


def slot_cuts(seq_count, capacity, head_count, compact):
    shapes = piece_shapes(head_count)
    counts = [row_count * col_count // (TS * TS) for row_count, col_count in shapes]
    attn_tiles = sum(counts[:5])
    sent_tiles = sum(counts[:7])
    cut_one = first_slots(attn_tiles, seq_count, capacity, 126) if compact else capacity
    cut_two = first_slots(sent_tiles, seq_count, capacity, 112) if compact else capacity
    spare = (seq_count, 2 * seq_count) if compact else (0, 0)
    return attn_tiles, sent_tiles, cut_one, cut_two, spare


def layout_plan(owner_row, seq_count, capacity, head_count):
    attn_tiles, sent_tiles, cut_one, cut_two, spare = slot_cuts(
        seq_count, capacity, head_count, True
    )
    tile_count = owner_row.shape[0]
    tile_ids = jnp.arange(tile_count, dtype=jnp.int32)
    onehot = (owner_row[:, None] == jnp.arange(seq_count, dtype=jnp.int32)[None, :]).astype(
        jnp.int32
    )
    before = jnp.cumsum(onehot, axis=0) - onehot
    rank = jnp.sum(before * onehot, axis=1)
    is_attn = tile_ids < attn_tiles
    is_sent = tile_ids < sent_tiles
    over = [is_attn & (rank >= cut_one), is_sent & ~is_attn & (rank >= cut_two)]
    over_place = [jnp.cumsum(which.astype(jnp.int32)) - 1 for which in over]
    fits = (
        (jnp.sum(over[0].astype(jnp.int32)) <= spare[0])
        & (jnp.sum(over[1].astype(jnp.int32)) <= spare[1])
        & (jnp.max(jnp.where(is_attn, rank, 0)) < first_pass_slot(cut_one, capacity))
    )
    return (
        fits,
        rank,
        over[0] | over[1],
        jnp.where(over[0], over_place[0], spare[0] + over_place[1]),
    )


def listed_tiles(owner_row, rank, devices, cut):
    tile_ids = jnp.arange(owner_row.shape[0], dtype=jnp.float32)
    by_owner = (owner_row[None, :] == devices[:, None]).astype(jnp.float32)
    by_rank = (rank[:, None] == jnp.arange(cut, dtype=jnp.int32)[None, :]).astype(jnp.float32)
    return jnp.dot(by_owner * tile_ids[None, :], by_rank, precision=PRECISE).astype(jnp.int32)


def tile_factors(local, cond_ref, spread_ref, chunk_ref):
    conds, width = spread_ref.shape
    chunks = width // conds
    start = local * TS
    top = start // chunks
    place = start - top * chunks + lax.broadcasted_iota(jnp.int32, (TS, 1), 0)
    row_at = jnp.zeros((TS, 1), jnp.int32)
    for later in range(1, (TS + chunks - 2) // chunks + 1):
        row_at += (place >= later * chunks).astype(jnp.int32)
    chunk_at = place - row_at * chunks
    rows = 8 * ((TS + chunks - 2) // chunks // 8 + 1)
    picked = cond_ref[pl.ds(top, rows), :].astype(jnp.bfloat16)
    select = (row_at == lax.broadcasted_iota(jnp.int32, (TS, rows), 1)).astype(jnp.bfloat16)
    factor = jnp.dot(select, picked, preferred_element_type=jnp.float32).astype(jnp.bfloat16)
    wide = jnp.dot(factor, spread_ref[...], preferred_element_type=jnp.float32)
    return jnp.where(chunk_at == chunk_ref[...], wide, 0.0).astype(jnp.bfloat16)


def factor_tables(cond_rows, mod_cols):
    conds, chunks = cond_rows.shape[0], mod_cols // TS
    rows = 8 * ((TS + chunks - 2) // chunks // 8 + 1)
    columns = np.arange(conds * chunks)
    spread = (columns[None, :] % conds == np.arange(conds)[:, None]).astype(np.float32)
    return (
        jnp.pad(cond_rows.T.astype(jnp.float32), ((0, rows), (0, 0))),
        jnp.array(spread, jnp.bfloat16),
        jnp.array(columns[None, :] // conds, jnp.int32),
    )


def mod_product(tables, master, first_slot, slot_count, local):
    width = tables[1].shape[1]

    def kernel(meta_ref, local_ref, cond_ref, spread_ref, chunk_ref, master_ref, out, land, sems):
        first, count = meta_ref[0], meta_ref[1]

        def tile_copy(at):
            slot = lax.rem(at, 2)
            return pltpu.make_async_copy(master_ref.at[first + at], land.at[slot], sems.at[slot])

        out[...] = jnp.zeros_like(out)

        @pl.when(count > 0)
        def _():
            tile_copy(0).start()

        def one(at, carry):
            @pl.when(at + 1 < count)
            def _():
                tile_copy(at + 1).start()

            tile_copy(at).wait()
            factors = tile_factors(local_ref[first + at], cond_ref, spread_ref, chunk_ref)
            out[...] += lax.dot_general(
                factors,
                land[lax.rem(at, 2)].astype(jnp.bfloat16),
                (((0,), (0,)), ((), ())),
                preferred_element_type=jnp.float32,
            )
            return carry

        lax.fori_loop(0, count, one, 0)

    whole = pl.BlockSpec(memory_space=pltpu.VMEM)
    return pl.pallas_call(
        kernel,
        out_shape=jax.ShapeDtypeStruct((width, TS), jnp.float32),
        grid_spec=pltpu.PrefetchScalarGridSpec(
            num_scalar_prefetch=2,
            grid=(1,),
            in_specs=[whole, whole, whole, pl.BlockSpec(memory_space=pl.ANY)],
            out_specs=whole,
            scratch_shapes=[pltpu.VMEM((2, TS, TS), jnp.float32), pltpu.SemaphoreType.DMA((2,))],
        ),
        compiler_params=pltpu.CompilerParams(
            dimension_semantics=("arbitrary",), vmem_limit_bytes=VMEM_BYTES
        ),
        cost_estimate=pl.CostEstimate(
            flops=80 * width * TS * TS, bytes_accessed=40 * 4 * TS * TS, transcendentals=0
        ),
        name="mod_product",
    )(jnp.stack([first_slot, slot_count]), local, *tables, master)


def adam_slots(
    begin, skipped, into, tables, dmod, local, kind_of, over_at, rate, sums, over_sums, *state
):
    capacity = state[0].shape[0]
    per = adam_block(capacity)

    def block_at(step, skip_ref):
        block = step + begin // per
        return jnp.where(
            (block >= skip_ref[0]) & (block < skip_ref[1]),
            jnp.where(skip_ref[1] < capacity // per, skip_ref[1], skip_ref[0] - 1),
            block,
        )


    def kernel(*refs):
        skip_ref, local_ref, kind_ref, over_ref, rate_ref = refs[:5]
        cond_ref, spread_ref, chunk_ref, dmod_ref, over_sums_ref, sums_ref = refs[5:11]
        master_ref, first_ref, second_ref = refs[11:14]
        *outs, grad_ref = refs[-4:]
        step = pl.program_id(0)
        block = block_at(step, skip_ref)
        is_new = (step == 0) | (block != block_at(step - 1, skip_ref))
        for at in range(per):
            slot = block * per + at
            kind = jnp.where(is_new, kind_ref[slot], -1)

            @pl.when(kind == 0)
            def _():
                grad_ref[...] = jnp.zeros_like(grad_ref)

            @pl.when(kind == 1)
            def _():
                grad_ref[...] = sums_ref[at].astype(jnp.float32)

            @pl.when(kind == 2)
            def _():
                grad_ref[...] = over_sums_ref[over_ref[slot]].astype(jnp.float32)

            @pl.when(kind == 3)
            def _():
                factors = tile_factors(local_ref[slot], cond_ref, spread_ref, chunk_ref)
                grad_ref[...] = jnp.dot(
                    factors, dmod_ref[...].astype(jnp.bfloat16), preferred_element_type=jnp.float32
                )

            @pl.when(is_new)
            def _():
                results = adam_step(
                    master_ref[at], first_ref[at], second_ref[at], grad_ref[...], rate_ref[slot]
                )
                for out, result in zip(outs, results):
                    out[at] = result

    whole = pl.BlockSpec(memory_space=pltpu.VMEM)
    block = pl.BlockSpec((per, TS, TS), lambda i, skip_ref, *_: (block_at(i, skip_ref), 0, 0))
    return pl.pallas_call(
        kernel,
        out_shape=[jax.ShapeDtypeStruct(state[0].shape, jnp.float32)] * 3,
        grid_spec=pltpu.PrefetchScalarGridSpec(
            num_scalar_prefetch=5,
            grid=((capacity - begin) // per,),
            in_specs=[whole] * 5
            + [block] * 4
            + [pl.BlockSpec(memory_space=pl.ANY)] * len(into),
            out_specs=[block] * 3,
            scratch_shapes=[pltpu.VMEM((TS, TS), jnp.float32)],
        ),
        input_output_aliases={14 + number: number for number in range(len(into))},
        compiler_params=pltpu.CompilerParams(
            dimension_semantics=("arbitrary",), vmem_limit_bytes=VMEM_BYTES
        ),
        cost_estimate=pl.CostEstimate(
            flops=80 * spread_flops(tables),
            bytes_accessed=13 * (capacity + begin) * TS * TS,
            transcendentals=0,
        ),
        name="adam_slots",
    )(
        jnp.stack(skipped).astype(jnp.int32),
        local,
        kind_of,
        over_at,
        rate,
        *tables,
        dmod,
        over_sums,
        sums,
        *state,
        *into,
    )


def spread_flops(tables):
    return tables[1].shape[1] * TS * TS


def windowed(queries, keys, values, allowed, local_heads):
    micro_count, row_count = queries.shape[:2]
    query_heads = queries.reshape(micro_count, row_count, local_heads, HD)
    key_heads = keys.reshape(micro_count, -1, local_heads, HD)
    value_heads = values.reshape(micro_count, -1, local_heads, HD)
    scores = jnp.einsum(
        "mqhd,mkhd->mhqk", query_heads, key_heads, preferred_element_type=jnp.float32
    ) * HD ** (-0.5)
    scores = jnp.where(allowed[:, None], scores, MASKED)
    highest = jnp.max(scores, axis=-1, keepdims=True)
    expo = jnp.exp(scores - highest)
    total = jnp.sum(expo, axis=-1, keepdims=True)
    probs = (expo / total).astype(jnp.bfloat16)
    result = jnp.einsum("mhqk,mkhd->mqhd", probs, value_heads, preferred_element_type=jnp.float32)
    return (
        result.reshape(micro_count, row_count, -1).astype(jnp.bfloat16),
        highest + jnp.log(total),
    )


def windowed_back(queries, keys, values, allowed, log_total, grad_out, local_heads):
    micro_count, row_count = queries.shape[:2]
    scale = HD ** (-0.5)
    query_heads = queries.reshape(micro_count, row_count, local_heads, HD)
    key_heads = keys.reshape(micro_count, -1, local_heads, HD)
    value_heads = values.reshape(micro_count, -1, local_heads, HD)
    grad_heads = grad_out.reshape(micro_count, row_count, local_heads, HD)
    key_count = keys.shape[1]
    scores = (
        jnp.einsum("mqhd,mkhd->mhqk", query_heads, key_heads, preferred_element_type=jnp.float32)
        * scale
    )
    probs = jnp.where(allowed[:, None], jnp.exp(scores - log_total), 0.0)
    dprobs = jnp.einsum(
        "mqhd,mkhd->mhqk", grad_heads, value_heads, preferred_element_type=jnp.float32
    )
    dscores = (probs * (dprobs - jnp.sum(probs * dprobs, axis=-1, keepdims=True))).astype(
        jnp.bfloat16
    )
    dquery = (
        jnp.einsum("mhqk,mkhd->mqhd", dscores, key_heads, preferred_element_type=jnp.float32)
        * scale
    )
    dkey = (
        jnp.einsum("mhqk,mqhd->mkhd", dscores, query_heads, preferred_element_type=jnp.float32)
        * scale
    )
    dvalue = jnp.einsum(
        "mhqk,mqhd->mkhd",
        probs.astype(jnp.bfloat16),
        grad_heads,
        preferred_element_type=jnp.float32,
    )
    return (
        dquery.reshape(micro_count, row_count, -1),
        dkey.reshape(micro_count, key_count, -1),
        dvalue.reshape(micro_count, key_count, -1),
    )


def matmul(left, right):
    return jnp.dot(left, right, preferred_element_type=jnp.float32)


def one_step(
    compact,
    x_in,
    cotangent,
    cond,
    context,
    clip_lengths,
    pad_mask,
    owners,
    master,
    first_moment,
    second_moment,
    rank,
    over,
    over_place,
    second_step,
):
    seq_count = lax.axis_size("seq")
    head_count = lax.axis_size("head")
    me = lax.axis_index("seq")
    capacity = master.shape[1]
    micro_count, row_count = x_in.shape[:2]
    frames = pad_mask.shape[1]
    clip_count = clip_lengths.shape[1]
    head_cols = D // head_count
    ff_cols = FF // head_count
    mod_cols = 6 * D // head_count
    local_heads = head_cols // HD
    first_row = me * row_count
    token_count = micro_count * row_count
    clip_span = min(clip_count, row_count // MINLEN + 2)
    shapes = piece_shapes(head_count)

    owner_row = owners[0]
    cuts = slot_cuts(seq_count, capacity, head_count, compact)
    attn_tiles, sent_tiles, cut_one, cut_two, spare = cuts
    tile_ids = jnp.arange(owner_row.shape[0], dtype=jnp.int32)
    over_hit = over[None, :] & (
        over_place[None, :] == jnp.arange(sum(spare), dtype=jnp.int32)[:, None]
    )
    over_tile = jnp.sum(jnp.where(over_hit, tile_ids[None, :], 0), axis=1)
    over_mine = jnp.any(over_hit & (owner_row == me)[None, :], axis=1)
    slot_hit = (owner_row[None, :] == me) & (
        rank[None, :] == jnp.arange(capacity, dtype=jnp.int32)[:, None]
    )
    slot_used = jnp.any(slot_hit, axis=1)
    slot_tile = jnp.sum(jnp.where(slot_hit, tile_ids[None, :], 0), axis=1)
    slot_tile = jnp.where(slot_used, slot_tile, -1)

    own = master[0]
    sizes = ring_sizes(seq_count)
    offsets = [0]
    for row_total, col_total in shapes[:7]:
        offsets.append(offsets[-1] + row_total * col_total // (TS * TS))
    inner = [math.prod(sizes[dim + 1 :]) for dim in range(3)]
    back = [(me // inner[dim] - owner_row // inner[dim]) % sizes[dim] for dim in range(3)]
    over_rank = jnp.sum(jnp.where(over_hit, rank[None, :], 0), axis=1)
    steps_back = [
        (me // inner[dim] - jnp.arange(sizes[dim], dtype=jnp.int32)) % sizes[dim] * inner[dim]
        for dim in range(3)
    ]
    devices = (
        steps_back[0][:, None, None] + steps_back[1][None, :, None] + steps_back[2][None, None, :]
    ).reshape(-1)

    def by_home(listed):
        return listed.reshape(seq_count, -1)[devices].reshape(*sizes, -1)

    def home_of(place, each):
        device = place // each
        steps = [(me // inner[dim] - device // inner[dim]) % sizes[dim] for dim in range(3)]
        return steps, place - device * each

    ticks = Ticks()
    chunks = [(0, cut_one), (cut_one, cut_two)]
    gather_parts = [portions(*chunk, wide) for chunk, wide in zip(chunks, GATHER_WIDE)]
    scatter_parts = [portions(*chunk, 34) for chunk in chunks]
    if compact:

        def start_pair(number, *parts, shift=0.0):
            first, middle, second, _ = gather_parts[number]
            block = (own[first:second] + shift).astype(jnp.bfloat16)
            ticks.start(("pair", number), gather_pair([block, *parts], middle - first, sizes))

        def start_rest(number, *extra, shift=0.0):
            block = own[gather_parts[number][2] : gather_parts[number][3]]
            block = (block + shift).astype(jnp.bfloat16)
            block = jnp.concatenate([block, *extra], axis=0)
            ticks.start(("rest", number), gather_ticks(block, sizes, (2, 1, 0)))

        start_pair(0, second_step)
        over_low = jnp.where(
            by_home(over_mine)[..., None, None],
            own[by_home(over_rank)].astype(jnp.bfloat16),
            jnp.zeros((), jnp.bfloat16),
        ).transpose(2, 1, 0, 3, 4, 5)
        ticks.start("over", scatter_ticks(lambda step: over_low[step], sizes, (2, 1, 0)))
        start_rest(0, ticks.finish(["over"])[0])
        for _ in range(sizes[0] - 2):
            ticks.tick([("pair", 0)])
        on_plane = ticks.moving["pair", 0]
        ticks.tick([("pair", 0)])
        start_pair(1, shift=nothing(*on_plane).astype(jnp.float32))
        on_plane = ticks.moving["pair", 0]
        ticks.finish([("pair", 0), ("rest", 0)])
        start_rest(1, shift=nothing(*on_plane).astype(jnp.float32))

    cond_rows = cond.reshape(micro_count * clip_count, D)
    tables = factor_tables(cond_rows, mod_cols)
    local = jnp.maximum(slot_tile - sent_tiles, 0)
    is_mod = slot_tile >= sent_tiles
    mod_count = jnp.sum(is_mod.astype(jnp.int32))
    tiles_here = jnp.sum((owner_row == me).astype(jnp.int32))
    mod_part = mod_product(tables, own, tiles_here - mod_count, mod_count, local)
    mod_part = (
        mod_part.reshape(mod_cols // TS, micro_count * clip_count, TS)
        .transpose(1, 0, 2)
        .reshape(micro_count * clip_count, mod_cols)
    )
    mod_all = lax.all_gather(lax.psum(mod_part, "seq"), "head", axis=1, tiled=True)

    weights = {}

    def fetch(kinds, numbers):
        if compact:
            each = sum(spare) // seq_count
            pools, source_at, index_at = [], jnp.zeros_like(rank), jnp.zeros_like(rank)
            steps, at = home_of(over_place, each)
            for number in numbers:
                first, middle, second, last = gather_parts[number]
                extra = 0 if number else each
                here = ~over & (rank >= second) & (rank < last)
                slot, block = rank - second, back
                if not number:
                    here = here | over
                    slot = jnp.where(over, last - second + at, slot)
                    block = [jnp.where(over, steps[dim], back[dim]) for dim in range(3)]
                source_at = jnp.where(here, len(pools) + block[0], source_at)
                index_at = jnp.where(
                    here, (block[1] * sizes[2] + block[2]) * (last - second + extra) + slot, index_at
                )
                pools = pools + ticks.results["rest", number]
                for which, (low, high, one, two) in enumerate(
                    [(first, middle, 2, 1), (middle, second, 1, 2)]
                ):
                    here = ~over & (rank >= low) & (rank < high)
                    array_at = back[one] * sizes[two] + back[two]
                    source_at = jnp.where(here, len(pools) + array_at, source_at)
                    index_at = jnp.where(here, back[0] * (high - low) + rank - low, index_at)
                    pools = pools + ticks.results["pair", number][which]
        else:
            pools = [lax.all_gather(own.astype(jnp.bfloat16), "seq", axis=0, tiled=True)]
            source_at = jnp.zeros_like(rank)
            index_at = owner_row * capacity + rank
        for kind in kinds:
            begin, end = offsets[kind : kind + 2]
            weights[kind] = fetch_matrix(
                pools, source_at[begin:end], index_at[begin:end], *shapes[kind]
            )

    if compact:
        fetch(range(5), [0])
    else:
        fetch(range(7), None)
    w_qkv, w_out, w_cq, w_ckv, w_cout = [weights[kind] for kind in range(5)]

    positions = first_row + jnp.arange(row_count, dtype=jnp.int32)
    ext_pos = first_row - WIN + jnp.arange(row_count + 2 * WIN, dtype=jnp.int32)
    near_keys, clip_keys, onehots, ctx_rows = [], [], [], []
    for micro_idx in range(micro_count):
        lengths = clip_lengths[micro_idx]
        clip_tok = clip_ids(lengths, positions)
        clip_start = jnp.minimum(clip_tok[0], clip_count - clip_span)
        key_clip = clip_start + jnp.arange(clip_span * CTX, dtype=jnp.int32) // CTX
        mask_pad = jnp.pad(pad_mask[micro_idx], (WIN, WIN))
        ext_flag = lax.dynamic_slice_in_dim(mask_pad, first_row, row_count + 2 * WIN, 0)
        near_keys.append(window_mask(positions, ext_pos, ext_flag, lengths, frames))
        clip_keys.append(clip_tok[:, None] == key_clip[None, :])
        listed = micro_idx * clip_count + clip_tok
        onehots.append(
            listed[:, None] == jnp.arange(micro_count * clip_count, dtype=jnp.int32)[None, :]
        )
        ctx_rows.append(
            lax.dynamic_slice_in_dim(context[micro_idx], clip_start, clip_span, 0).reshape(
                clip_span * CTX, DC
            )
        )
    near_keys, clip_keys = jnp.stack(near_keys), jnp.stack(clip_keys)
    onehot = jnp.concatenate(onehots, axis=0).astype(jnp.float32)
    ctx_rows = jnp.concatenate(ctx_rows, axis=0)

    def by_micro(rows):
        return rows.reshape(micro_count, -1, rows.shape[-1])

    def flat(rows):
        return rows.reshape(-1, rows.shape[-1])

    mod_frames = jnp.dot(onehot, mod_all, precision=PRECISE)
    shifts = [mod_frames[:, 2 * which * D : (2 * which + 1) * D] for which in range(3)]
    scales = [mod_frames[:, (2 * which + 1) * D : (2 * which + 2) * D] for which in range(3)]
    resid_zero = flat(x_in).astype(jnp.float32)
    normed_one, inverse_one = layer_norm(resid_zero)
    input_one = (normed_one * (1.0 + scales[0]) + shifts[0]).astype(jnp.bfloat16)
    second = [("pair", 1), ("rest", 1)] if compact else []
    proj_qkv = by_micro(matmul(input_one, w_qkv).astype(jnp.bfloat16))
    queries = proj_qkv[:, :, :head_cols]
    kv_ext = padded(proj_qkv[:, :, head_cols:], (("seq", 1),), WIN)
    attended, log_one = windowed(
        queries, kv_ext[:, :, :head_cols], kv_ext[:, :, head_cols:], near_keys, local_heads
    )
    resid_one = resid_zero + head_sum(matmul(flat(attended), w_out))
    normed_two, inverse_two = layer_norm(resid_one)
    input_two = (normed_two * (1.0 + scales[1]) + shifts[1]).astype(jnp.bfloat16)
    cross_query = by_micro(matmul(input_two, w_cq).astype(jnp.bfloat16))
    cross_kv = by_micro(matmul(ctx_rows, w_ckv).astype(jnp.bfloat16))
    cross_out, log_two = windowed(
        cross_query, cross_kv[:, :, :head_cols], cross_kv[:, :, head_cols:], clip_keys, local_heads
    )
    resid_two = resid_one + head_sum(matmul(flat(cross_out), w_cout))
    if compact:
        ticks.finish([("pair", 1), ("rest", 1)])
        fetch((6, 5), [0, 1])
    w_glu, w_down = weights[5], weights[6]
    normed_three, inverse_three = layer_norm(resid_two)
    input_three = (normed_three * (1.0 + scales[2]) + shifts[2]).astype(jnp.bfloat16)
    gate_up = matmul(input_three, w_glu)
    gate_part = gate_up[:, :ff_cols]
    up_part = gate_up[:, ff_cols:]
    sigmoid_gate = jax.nn.sigmoid(gate_part)
    silu_gate = gate_part * sigmoid_gate
    hidden = (silu_gate * up_part).astype(jnp.bfloat16)

    grad_low = flat(cotangent)
    grad_three = grad_low.astype(jnp.float32)
    pool_ff = as_tiles(matmul(hidden.T, grad_low), sent_tiles, offsets[6])
    grad_hidden = matmul(grad_low, w_down.T)
    dglu = jnp.concatenate(
        [
            grad_hidden * up_part * sigmoid_gate * (1.0 + gate_part * (1.0 - sigmoid_gate)),
            grad_hidden * silu_gate,
        ],
        axis=1,
    ).astype(jnp.bfloat16)
    pool_ff = as_tiles(matmul(input_three.T, dglu), pool_ff, offsets[5])
    slots = listed_tiles(owner_row, rank, devices, cut_two)

    def start_scatter(number, pool, listed, extra=None, before=()):
        first, middle, second, last = scatter_parts[number]
        wanted = jnp.concatenate(
            [slots.reshape(*sizes, cut_two), by_home(listed)], axis=3
        )
        if number:
            wanted = jnp.maximum(wanted, attn_tiles)
        home = wanted[..., cut_two:]
        planes = [
            (wanted[..., first:middle].transpose(2, 1, 0, 3), 2),
            (wanted[..., middle:second].transpose(1, 2, 0, 3), 1),
            (jnp.concatenate([wanted[..., second:last], home], axis=3), 0),
        ]

        def pick(parts, *before):
            flats = [part.reshape(-1) for part in parts]
            tiles = pool[jnp.concatenate(flats) + nothing(*before)]
            edges = np.cumsum([0] + [flat.shape[0] for flat in flats])
            return [
                tiles[edges[at] : edges[at + 1]].reshape(*part.shape, TS, TS)
                for at, part in enumerate(parts)
            ]

        sent = pick([places[1] for places, _ in planes])
        kept = [jnp.concatenate([places[:1], places[2:]]) for places, _ in planes]
        kept = pick(kept, sent[0], *before)
        taken = sent + kept
        if extra is not None:
            sent[2] = jnp.concatenate([sent[2], extra[1]], axis=2)
            kept[2] = jnp.concatenate([kept[2], jnp.concatenate([extra[:1], extra[2:]])], axis=3)
        parts = [[kept[at][0], sent[at], *kept[at][1:]] for at in range(3)]
        one, two, three = parts
        ticks.start(("pair", number), scatter_pair(one, two, sizes))
        ticks.start(
            ("rest", number),
            scatter_ticks(lambda step: three[step], sizes, (0, 1, 2)),
        )
        return taken

    def hand_out():
        totals = [
            ticks.finish([("rest", number)])[0][scatter_parts[number][3] - scatter_parts[number][2] :]
            for number in range(2)
        ]
        block = jnp.concatenate(totals, axis=0)
        ticks.start("out", gather_ticks(block, sizes, (0, 1, 2)))
        return jnp.concatenate(ticks.finish(["out"])[0], axis=0)

    if compact:
        taken = start_scatter(1, pool_ff, over_tile[spare[0] :])
        pool_ff, _ = lax.optimization_barrier((pool_ff, taken))
    back_three, dscale_three, dshift_three = norm_back(
        head_sum(matmul(dglu, w_glu.T)), normed_three, inverse_three, scales[2]
    )
    grad_two = grad_three + back_three
    grad_low = grad_two.astype(jnp.bfloat16)
    grad_cout = matmul(flat(cross_out).T, grad_low).astype(jnp.bfloat16)
    grad_cross = by_micro(matmul(grad_low, w_cout.T).astype(jnp.bfloat16))
    dquery_two, dkey_two, dvalue_two = windowed_back(
        cross_query,
        cross_kv[:, :, :head_cols],
        cross_kv[:, :, head_cols:],
        clip_keys,
        log_two,
        grad_cross,
        local_heads,
    )
    dquery_two = flat(dquery_two).astype(jnp.bfloat16)
    pool = as_tiles(grad_cout, pool_ff, offsets[4])
    pool = as_tiles(matmul(input_two.T, dquery_two), pool, offsets[2])
    dkv_two = flat(jnp.concatenate([dkey_two, dvalue_two], axis=2)).astype(jnp.bfloat16)
    pool = as_tiles(matmul(ctx_rows.T, dkv_two), pool, offsets[3])
    back_two, dscale_two, dshift_two = norm_back(
        head_sum(matmul(dquery_two, w_cq.T)), normed_two, inverse_two, scales[1]
    )
    grad_one = ticks.tick(second[1:], grad_two + back_two)
    grad_low = grad_one.astype(jnp.bfloat16)
    pool = as_tiles(matmul(flat(attended).T, grad_low), pool, offsets[1])
    grad_attended = by_micro(matmul(grad_low, w_out.T).astype(jnp.bfloat16))
    dquery_one, dkey_ext, dvalue_ext = windowed_back(
        queries,
        kv_ext[:, :, :head_cols],
        kv_ext[:, :, head_cols:],
        near_keys,
        log_one,
        grad_attended,
        local_heads,
    )
    dkv_ext = ticks.tick(second, jnp.concatenate([dkey_ext, dvalue_ext], axis=2))
    rims = jnp.concatenate([dkv_ext[:, :WIN], dkv_ext[:, row_count + WIN :]], axis=1)
    returned = padded(rims.astype(jnp.bfloat16), (("seq", 1),), WIN).astype(jnp.float32)
    dkv_own = dkv_ext[:, WIN : row_count + WIN]
    dkv_own = dkv_own.at[:, :WIN].add(returned[:, :WIN])
    dkv_own = dkv_own.at[:, row_count - WIN :].add(returned[:, 3 * WIN :])
    dqkv = flat(jnp.concatenate([dquery_one, dkv_own], axis=2).astype(jnp.bfloat16))
    dqkv = ticks.tick(second, dqkv)
    pool = as_tiles(matmul(input_one.T, dqkv), pool, offsets[0])
    back_one, dscale_one, dshift_one = norm_back(
        ticks.tick(second, head_sum(matmul(dqkv, w_qkv.T))), normed_one, inverse_one, scales[0]
    )
    grad_input = by_micro(grad_one + back_one)

    dmod = jnp.concatenate(
        [
            jnp.dot(onehot.T, rows, precision=PRECISE)
            for rows in (
                dshift_one,
                dscale_one,
                dshift_two,
                dscale_two,
                dshift_three,
                dscale_three,
            )
        ],
        axis=1,
    )
    dmod = lax.dynamic_slice_in_dim(dmod, lax.axis_index("head") * mod_cols, mod_cols, 1)
    dmod = (
        dmod.reshape(micro_count * clip_count, mod_cols // TS, TS)
        .transpose(1, 0, 2)
        .reshape(-1, TS)
    )
    gate = [dqkv]
    if compact:
        each = dmod.shape[0] // seq_count
        extra = dmod.astype(jnp.bfloat16).reshape(seq_count, each, TS)[devices]
        extra = jnp.pad(extra, ((0, 0), (0, TS - each), (0, 0))).reshape(*sizes, 1, TS, TS)
        ticks.tick(second)
        before = sum([ticks.moving[name] for name in second if name in ticks.running], [])
        gate = start_scatter(0, pool, over_tile[: spare[0]], extra, before)
    else:
        dmod = lax.psum(dmod, "seq")
    late = (hidden.astype(jnp.float32) + nothing(gate[0]).astype(jnp.float32)).astype(jnp.bfloat16)
    out_block = by_micro((resid_two + head_sum(matmul(late, w_down))).astype(jnp.bfloat16))
    state = (own, first_moment[0], second_moment[0])
    rate = slot_rates(slot_tile, shapes)
    if compact:
        over_slot = slot_hit & over[None, :]
        slot_over = jnp.any(over_slot, axis=1)
        over_at = jnp.sum(jnp.where(over_slot, over_place[None, :], 0), axis=1)
        kind_of = jnp.where(is_mod, 3, jnp.where(slot_over, 2, slot_used.astype(jnp.int32)))

        def sums_of(number):
            first, _, second, last = scatter_parts[number]
            pair, rest = ticks.finish([("pair", number), ("rest", number)])
            return [pair, rest[: last - second]]

        over_sums = hand_out()
        each = [count // seq_count for count in spare]
        width = sum(each) + 1

        def home_block(steps):
            return (steps[2] * sizes[1] + steps[1]) * sizes[0] + steps[0]

        homes = home_block(home_of(np.arange(seq_count), 1)[0])
        count = dmod.shape[0] // seq_count
        dmod = over_sums[homes * width + each[0], :count].reshape(dmod.shape)
        steps, at = home_of(over_at, each[0])
        index = home_block(steps) * width + at
        steps, at = home_of(over_at - spare[0], each[1])
        other = home_block(steps) * width + each[0] + 1 + at
        index = jnp.where(over_at < spare[0], index, other)
        results = adam_slots(
            0,
            (jnp.int32(0), jnp.int32(0)),
            (),
            tables,
            dmod.astype(jnp.float32),
            local,
            kind_of,
            jnp.clip(index, 0, over_sums.shape[0] - 1),
            rate,
            jnp.concatenate(
                [
                    *sums_of(0),
                    *sums_of(1),
                    jnp.zeros((capacity - cut_two, TS, TS), jnp.bfloat16),
                ],
                axis=0,
            ),
            over_sums,
            *state,
        )
    else:
        sums = lax.psum_scatter(
            pool[listed_tiles(owner_row, rank, jnp.arange(seq_count), capacity).reshape(-1)],
            "seq",
            scatter_dimension=0,
            tiled=True,
        )
        results = adam_slots(
            0,
            (jnp.int32(0), jnp.int32(0)),
            (),
            tables,
            dmod,
            local,
            jnp.where(is_mod, 3, slot_used.astype(jnp.int32)),
            jnp.zeros_like(slot_tile),
            rate,
            sums,
            jnp.zeros((1, TS, TS), jnp.bfloat16),
            *state,
        )
    weight, first, second = results
    return (out_block, grad_input, weight[None], first[None], second[None])


def on_device(*args):
    owner_row, own = args[6][0], args[7][0]
    seq_count, capacity = lax.axis_size("seq"), own.shape[0]
    head_count = lax.axis_size("head")
    first, _, second, _ = portions(
        0, slot_cuts(seq_count, capacity, head_count, True)[2], GATHER_WIDE[0]
    )
    block = own[first:second].astype(jnp.bfloat16)
    second_step = ring_send(block, ring_sizes(seq_count), 0)
    fits, *plan = layout_plan(owner_row, seq_count, capacity, head_count)
    misfits = lax.pmax(1 - fits.astype(jnp.int32), "head")
    return lax.cond(
        misfits == 0, partial(one_step, True), partial(one_step, False), *args, *plan, second_step
    )


def solution(mesh):
    placed = (
        P(None, "seq", None),
        P(None, "seq", None),
        P(),
        P(),
        P(),
        P(),
        P("head", None),
        P("head", "seq", None, None),
        P("head", "seq", None, None),
        P("head", "seq", None, None),
    )
    return jax.shard_map(
        on_device,
        mesh=mesh,
        in_specs=placed,
        out_specs=(
            P(None, "seq", None),
            P(None, "seq", None),
            P("head", "seq", None, None),
            P("head", "seq", None, None),
            P("head", "seq", None, None),
        ),
        check_vma=False,
    )
```
